128 devices in a mesh: node: 16 (over z_lo, y, core), local: 8 (over x, z_hi).
Axes of the slice: x: 4, y: 4, z: 4 (z_hi: 2, z_lo: 2; z = z_hi * 2 + z_lo), core: 2. Of those that a mesh axis runs over, the one named last changes fastest.
Arguments:
- grad_out: bfloat16 [16384, 128, 384], P(('node', 'local')), may hold values from -24 to 24
- pooled: bfloat16 [16384, 128, 256], P(('node', 'local')), may hold values from -24 to 24
- proj: bfloat16 [128, 256, 128], P(('node', 'local')), may hold values from -0.5 to 0.5
- assign: int32 [128], replicated, may hold values from 0 to 127, each once
- indices: int32 [128, 16384, 3, 8], P(('node', 'local')), may hold values from 0 to 511
- lengths: int32 [128, 16384, 3], P(('node', 'local')), may hold values from 1 to 8
Outputs:
- table_grad: float32 [128, 512, 256], P(('node', 'local'))
- proj_grad: float32 [128, 256, 128], P(('node', 'local'))
The draws below stay inside these ranges and needn't reach their ends.
Inputs may be any that keep to these rules, and one draw needn't show every extreme that they name: assign holds every group id once.
All inputs are finite; a program needn't handle non-finite values.
Results may differ from the reference program's by a relative error of at most 0.0029.
Values may be sent and summed in bfloat16 or wider, within the bound.
A program may use at most 192 MiB of HBM per device.

```python
import math
import jax
import jax.numpy as jnp
import numpy as np
from jax import lax

ROWS = 512
BAG = 8
W1 = 16
W2 = 48
W3 = 192
PD = 128
WSUM = 256
CAT = 384
GROUPS = 128
BATCH = 16384


def with_ends(result, rng, smallest, high):
    place = [jax.random.randint(jax.random.fold_in(rng, axis), (), 0, length) for axis, length in enumerate(result.shape)]
    widest = result.shape.index(max(result.shape))
    beside = place[:widest] + [(place[widest] + 1) % result.shape[widest]] + place[widest + 1:]
    return result.at[tuple(place)].set(smallest).at[tuple(beside)].set(high)


def raised(drawn, key, source, target, parts, factor):
    def block_of(position):
        return (jnp.arange(drawn.shape[position]) // (drawn.shape[position] // parts)).reshape((-1,) + (1,) * (drawn.ndim - 1 - position))

    one_side = jax.random.permutation(key, parts)[block_of(target)]
    second = (block_of(target) + parts // 2) % parts
    return jnp.where((block_of(source) == one_side) | (block_of(source) == second), factor * drawn, drawn)


def levels(stream_key, dims, pieces, low, high):
    def one(axis_at, shards_of):
        heights = jax.random.uniform(jax.random.fold_in(jax.random.fold_in(stream_key, 6), axis_at), (shards_of,), jnp.float32, low / len(pieces), high / len(pieces))
        return jnp.repeat(jnp.exp(heights), dims[axis_at] // shards_of).reshape((-1,) + (1,) * (len(dims) - axis_at - 1))

    loudness = one(*pieces[0])
    for cut in pieces[1:]:
        loudness = loudness * one(*cut)
    return loudness


def rank_table(number_of, lean):
    loads = [(1 << 20) // math.isqrt(standing ** lean) + 1 for standing in range(1, number_of + 1)]
    scale = 1 + sum(loads) // (1 << 30)
    return np.cumsum(np.array([max(1, weight // scale) for weight in loads]))


def ranked(key, dims, amount, lean):
    table = rank_table(amount, lean)
    lot = jax.random.randint(jax.random.fold_in(key, 1), dims, 0, int(table[amount - 1]))
    grade = jnp.searchsorted(jnp.asarray(table, jnp.int32), lot, side="right")
    return jax.random.permutation(jax.random.fold_in(key, 2), amount)[grade].astype(jnp.int32)


def gaussian(stream_key, shape, scale, reach, shards=(), kind=jnp.bfloat16):
    result = jax.random.normal(stream_key, shape, jnp.float32) * scale
    if len(shards) > 0:
        result = levels(stream_key, shape, shards, -0.22, 0.18) * result
    return jnp.clip(result, min=-reach, max=reach).astype(kind)


def bell_draw_with(rng, extent, scale, reach, shards, heavy, held_as=jnp.bfloat16):
    result = scale * jax.random.normal(rng, extent, jnp.float32)
    if shards:
        result = result * levels(rng, extent, shards, -0.22, 0.18)
    return jnp.clip(raised(result, jax.random.fold_in(rng, 3), *heavy), -reach, reach).astype(held_as)


def setup_inputs(seed: int = 0) -> dict:
    seeds = jax.random.split(jax.random.key(seed), 7)
    grad_out = bell_draw_with(seeds[0], (BATCH, GROUPS, CAT), 1.0, 24.0, ((0, 128),), (0, 1, 128, 5.5))
    pooled = bell_draw_with(seeds[1], (BATCH, GROUPS, WSUM), 1.0, 24.0, ((0, 128),), (0, 1, 128, 5.5))
    proj = gaussian(seeds[2], (GROUPS, WSUM, PD), PD ** -0.5, 0.5, ((0, 128),))
    assign = jax.random.permutation(seeds[3], GROUPS).astype(jnp.int32)
    indices = with_ends(ranked(seeds[4], (GROUPS, BATCH, 3, BAG), ROWS, 2), jax.random.fold_in(seeds[4], 3), 0, ROWS - 1).astype(jnp.int32)
    lengths = with_ends(jax.random.randint(seeds[5], (GROUPS, BATCH, 3), 1, BAG + 1), jax.random.fold_in(seeds[5], 1), 1, BAG).astype(jnp.int32)
    return {"grad_out": grad_out, "pooled": pooled, "proj": proj, "assign": assign, "indices": indices, "lengths": lengths}


def reference(grad_out, pooled, proj, assign, indices, lengths):
    widths = (W1, W2, W3)
    scale = 1.0 / math.sqrt(BATCH)

    def one_slot(slot):
        group = assign[slot]
        grads = lax.dynamic_index_in_dim(grad_out, group, 1, keepdims=False)
        saved = lax.dynamic_index_in_dim(pooled, group, 1, keepdims=False)
        weights = proj[slot]
        lookups = indices[slot]
        counts = lengths[slot]
        tables = []
        projections = []
        offset = 0
        for table, width in enumerate(widths):
            grad_part = grads[:, table * PD:(table + 1) * PD]
            rounded = jnp.dot(grad_part, weights[offset:offset + width].T, preferred_element_type=jnp.float32).astype(jnp.bfloat16)
            dpool = lax.optimization_barrier(rounded).astype(jnp.float32)
            projections.append(jnp.dot(saved[:, offset:offset + width].T, grad_part, preferred_element_type=jnp.float32) * scale)
            total = jnp.zeros((ROWS, width), jnp.float32)
            for lookup in range(BAG):
                keep = (counts[:, table] > lookup).astype(jnp.float32)
                total = total + jax.ops.segment_sum(dpool * keep[:, None], lookups[:, table, lookup], num_segments=ROWS)
            tables.append(total)
            offset = offset + width
        return (jnp.concatenate(tables, axis=1), jnp.concatenate(projections, axis=0))
    table_grad, proj_grad = lax.map(one_slot, jnp.arange(GROUPS, dtype=jnp.int32))
    return (table_grad, proj_grad)
```

```python
import functools
import math

import jax
import jax.numpy as jnp
from jax import lax
from jax.experimental import pallas as pl
from jax.experimental.pallas import tpu as pltpu
from jax.sharding import PartitionSpec as P

ROWS = 512
W1 = 16
W2 = 48
W3 = 192
W12 = W1 + W2
WSUM = W12 + W3
PD = 128
BAG = 8
SLOTS = 128
PER = 16
BANDS = ((0, 96), (96, 80), (176, 80))
ORDERS = (("z", "y", "x"), ("y", "x", "z"), ("x", "z", "y"))
BF = jnp.bfloat16
F32 = jnp.float32
MINOR = (((1,), (1,)), ((), ()))
MAJOR = (((0,), (0,)), ((), ()))


def coords(node, local):
    return {
        "core": node % 2,
        "y": node // 2 % 4,
        "x": local // 2,
        "z": local % 2 * 2 + node // 8,
    }


def place(at):
    return {
        "node": (at["z"] % 2 * 4 + at["y"]) * 2 + at["core"],
        "local": at["x"] * 2 + at["z"] // 2,
    }


def prepare_kernel(
    pos_ref, g_ref, q_ref, w_ref, send_ref, b0_ref, b1_ref, b2_ref, gt, qt, stage, pstage, ssem, psem, *, steps
):
    step = pl.program_id(0)
    now = lax.rem(step, 2)
    bands = (b0_ref, b1_ref, b2_ref)

    def drain(half):
        pltpu.make_async_copy(stage.at[half], stage.at[half], ssem.at[half]).wait()
        pltpu.make_async_copy(pstage.at[half], pstage.at[half], psem.at[half]).wait()

    @pl.when(step >= 2)
    def _():
        drain(now)

    gt[...] = jnp.swapaxes(g_ref[...], 0, 1)
    qt[...] = jnp.swapaxes(q_ref[...], 0, 1)

    def one(k, carry):
        group = step * PER + k
        slot = pos_ref[0, group]
        g = gt[k]
        q = qt[k]
        w = w_ref[slot]
        d1 = lax.dot_general(w[0:W1], g[:, 0:PD], MINOR, preferred_element_type=F32)
        d2 = lax.dot_general(w[W1:W12], g[:, PD : 2 * PD], MINOR, preferred_element_type=F32)
        stage[now, k, 0:PD] = g[:, 2 * PD : 3 * PD]
        stage[now, k, PD : PD + W1] = d1.astype(BF)
        stage[now, k, PD + W1 : PD + W12] = d2.astype(BF)
        third = lax.dot_general(q, g[:, 2 * PD : 3 * PD], MAJOR, preferred_element_type=F32)
        both = lax.dot_general(q[:, 0:W12], g[:, 0 : 2 * PD], MAJOR, preferred_element_type=F32)
        pstage[now, k, 0:W1] = both[0:W1, 0:PD]
        pstage[now, k, W1:W12] = both[W1:W12, PD : 2 * PD]
        pstage[now, k, W12:WSUM] = third[W12:WSUM]
        pltpu.make_async_copy(stage.at[now, k], send_ref.at[slot], ssem.at[now]).start()
        for n, (at, rows) in enumerate(BANDS):
            pltpu.make_async_copy(
                pstage.at[now, k, pl.ds(at, rows)], bands[n].at[pos_ref[1 + n, group]], psem.at[now]
            ).start()
        return carry

    lax.fori_loop(0, PER, one, 0, unroll=4)

    @pl.when(step == steps - 1)
    def _():
        drain(1 - now)
        drain(now)


def prepare(pos, grad_out, pooled, w12):
    count = grad_out.shape[0]
    steps = SLOTS // PER
    return pl.pallas_call(
        functools.partial(prepare_kernel, steps=steps),
        grid_spec=pltpu.PrefetchScalarGridSpec(
            num_scalar_prefetch=1,
            grid=(steps,),
            in_specs=[
                pl.BlockSpec((count, PER, 3 * PD), lambda i, p: (0, i, 0)),
                pl.BlockSpec((count, PER, WSUM), lambda i, p: (0, i, 0)),
                pl.BlockSpec((SLOTS, W12, PD), lambda i, p: (0, 0, 0)),
            ],
            out_specs=[pl.BlockSpec(memory_space=pl.ANY)] * 4,
            scratch_shapes=[
                pltpu.VMEM((PER, count, 3 * PD), BF),
                pltpu.VMEM((PER, count, WSUM), BF),
                pltpu.VMEM((2, PER, PD + W12, count), BF),
                pltpu.VMEM((2, PER, WSUM, PD), F32),
                pltpu.SemaphoreType.DMA((2,)),
                pltpu.SemaphoreType.DMA((2,)),
            ],
        ),
        out_shape=[jax.ShapeDtypeStruct((SLOTS, PD + W12, count), BF)]
        + [jax.ShapeDtypeStruct((SLOTS, rows, PD), F32) for _, rows in BANDS],
        compiler_params=pltpu.CompilerParams(vmem_limit_bytes=48 * 2**20),
        cost_estimate=pl.CostEstimate(flops=4 * 10**9, bytes_accessed=50 * 10**6, transcendentals=0),
    )(pos, grad_out, pooled, w12)


def reduce_kernel(scale, *refs):
    bands, out_ref = refs[0:3], refs[3]
    own, got, s1, r1, t, r2, u, r3 = (refs[4 + 3 * n : 7 + 3 * n] for n in range(8))
    own_sem, core_sem, sem1, sem2, sem3 = refs[28:33]
    me = coords(lax.axis_index("node"), lax.axis_index("local"))
    core = me["core"]

    def other(axis, hop):
        size = 2 if axis == "core" else 4
        return place(dict(me, **{axis: (me[axis] + hop) % size}))

    partners = [other("core", 1)] + [other(axis, hop) for axis in "xyz" for hop in (1, 2, 3)]
    barrier = pltpu.get_barrier_semaphore()
    for partner in partners:
        pl.semaphore_signal(barrier, inc=1, device_id=partner, device_id_type=pl.DeviceIdType.MESH)
    pl.semaphore_wait(barrier, len(partners))

    def send(src, dst, sems, at, to):
        copy = pltpu.make_async_remote_copy(
            src_ref=src,
            dst_ref=dst,
            send_sem=sems.at[(0,) + at],
            recv_sem=sems.at[(1,) + at],
            device_id=to,
            device_id_type=pl.DeviceIdType.MESH,
        )
        copy.start()
        return copy

    hops = (1, 2, 3, 0)
    loads, core_copies = {}, {}
    for hop in hops:
        for n in range(3):
            at = (me[ORDERS[n][0]] + hop) % 4 * 16
            loads[n, hop] = pltpu.make_async_copy(
                bands[n].at[pl.ds(core * 64 + at, 16)], own[n].at[hop], own_sem.at[n, hop]
            )
            loads[n, hop].start()
            core_copies[n, hop] = send(
                bands[n].at[pl.ds((1 - core) * 64 + at, 16)], got[n].at[hop], core_sem, (n, hop), other("core", 1)
            )

    first = {}
    for hop in hops:
        for n in range(3):
            loads[n, hop].wait()
            core_copies[n, hop].wait_recv()

            def add(i, carry):
                total = own[n][hop, i] + got[n][hop, i]
                if hop == 0:
                    t[n][i] = total
                else:
                    s1[n][hop - 1, i] = total.astype(BF)
                return carry

            lax.fori_loop(0, 16, add, 0)
            if hop:
                first[n, hop] = send(
                    s1[n].at[hop - 1], r1[n].at[hop - 1], sem1, (n, hop - 1), other(ORDERS[n][0], hop)
                )

    second = {}
    for n in range(3):
        for hop in (1, 2, 3):
            first[n, hop].wait_recv()

        def add(i, carry):
            t[n][i] = t[n][i] + (
                r1[n][0, i].astype(F32) + r1[n][1, i].astype(F32) + r1[n][2, i].astype(F32)
            )
            return carry

        lax.fori_loop(0, 16, add, 0)
        for hop in (1, 2, 3):
            at = (me[ORDERS[n][1]] + hop) % 4 * 4
            second[n, hop] = send(
                t[n].at[pl.ds(at, 4)], r2[n].at[hop - 1], sem2, (n, hop - 1), other(ORDERS[n][1], hop)
            )

    third = {}
    for n in range(3):
        for hop in (1, 2, 3):
            second[n, hop].wait_recv()
        at = me[ORDERS[n][1]] * 4

        def add(i, carry):
            u[n][i] = t[n][at + i] + (r2[n][0, i] + r2[n][1, i] + r2[n][2, i])
            return carry

        lax.fori_loop(0, 4, add, 0)
        for hop in (1, 2, 3):
            to = (me[ORDERS[n][2]] + hop) % 4
            third[n, hop] = send(u[n].at[to], r3[n].at[hop - 1], sem3, (n, hop - 1), other(ORDERS[n][2], hop))

    for n, (start, rows) in enumerate(BANDS):
        for hop in (1, 2, 3):
            third[n, hop].wait_recv()
        total = u[n][me[ORDERS[n][2]]] + (r3[n][0] + r3[n][1] + r3[n][2])
        out_ref[start : start + rows] = total * scale

    for copies in (core_copies, first, second, third):
        for copy in copies.values():
            copy.wait_send()


def reduce_bands(bands, scale):
    def each(*lead, kind=F32):
        return [pltpu.VMEM(lead + (rows, PD), kind) for _, rows in BANDS]

    return pl.pallas_call(
        functools.partial(reduce_kernel, scale),
        in_specs=[pl.BlockSpec(memory_space=pl.ANY)] * 3,
        out_specs=pl.BlockSpec(memory_space=pltpu.VMEM),
        out_shape=jax.ShapeDtypeStruct((WSUM, PD), F32),
        scratch_shapes=[
            *each(4, 16),
            *each(4, 16),
            *each(3, 16, kind=BF),
            *each(3, 16, kind=BF),
            *each(16),
            *each(3, 4),
            *each(4),
            *each(3),
            pltpu.SemaphoreType.DMA((3, 4)),
            pltpu.SemaphoreType.DMA((2, 3, 4)),
            pltpu.SemaphoreType.DMA((2, 3, 3)),
            pltpu.SemaphoreType.DMA((2, 3, 3)),
            pltpu.SemaphoreType.DMA((2, 3, 3)),
        ],
        compiler_params=pltpu.CompilerParams(
            collective_id=0, has_side_effects=True, vmem_limit_bytes=48 * 2**20
        ),
        cost_estimate=pl.CostEstimate(flops=10**7, bytes_accessed=40 * 10**6, transcendentals=0),
    )(*bands)


COLS = 512


def count_kernel(idx_ref, len_ref, out_ref):
    rows = lax.broadcasted_iota(jnp.int32, (64, 128), 0)
    order = lax.broadcasted_iota(jnp.int32, (BAG, 128), 0)

    def column(c, carry):
        at = pl.multiple_of(c * 128, 128)
        for table in range(3):
            idx = idx_ref[table, :, pl.ds(at, 128)]
            keep = order < len_ref[table : table + 1, pl.ds(at, 128)]
            low = idx & 63
            unit = jnp.where(keep, lax.shift_left(jnp.ones_like(idx), 4 * lax.shift_right_logical(idx, 6)), 0)
            total = jnp.zeros((64, 128), jnp.int32)
            for j in range(BAG):
                total = total + jnp.where(low[j : j + 1] == rows, unit[j : j + 1], 0)
            for part in range(8):
                count = lax.shift_right_logical(total, 4 * part) & 15
                out_ref[table, 64 * part : 64 * part + 64, pl.ds(at, 128)] = count.astype(F32).astype(BF)
        return carry

    lax.fori_loop(0, COLS // 128, column, 0)


def count_rows(lookups, lengths):
    total = lookups.shape[2]
    return pl.pallas_call(
        count_kernel,
        grid=(total // COLS,),
        in_specs=[
            pl.BlockSpec((3, BAG, COLS), lambda i: (0, 0, i)),
            pl.BlockSpec((3, COLS), lambda i: (0, i)),
        ],
        out_specs=pl.BlockSpec((3, ROWS, COLS), lambda i: (0, 0, i)),
        out_shape=jax.ShapeDtypeStruct((3, ROWS, total), BF),
        compiler_params=pltpu.CompilerParams(vmem_limit_bytes=32 * 2**20),
        cost_estimate=pl.CostEstimate(flops=4 * 10**9, bytes_accessed=60 * 10**6, transcendentals=0),
    )(lookups, lengths)


SOURCES = 8


def table_kernel(hits_ref, got_ref, w_ref, out_ref, a1, a2, a3):
    step = pl.program_id(0)

    @pl.when(step == 0)
    def _():
        a1[...] = jnp.zeros_like(a1)
        a2[...] = jnp.zeros_like(a2)
        a3[...] = jnp.zeros_like(a3)

    wide = got_ref[:, 0:PD, :].reshape(SOURCES * PD, PD)
    narrow = jnp.concatenate([got_ref[s, PD : PD + W12, :] for s in range(SOURCES)], axis=1)
    a1[...] += lax.dot_general(hits_ref[0], narrow[0:W1], MINOR, preferred_element_type=F32)
    a2[...] += lax.dot_general(hits_ref[1], narrow[W1:W12], MINOR, preferred_element_type=F32)
    a3[...] += jnp.dot(hits_ref[2], wide, preferred_element_type=F32)

    @pl.when(step == pl.num_programs(0) - 1)
    def _():
        total = a3[...]
        high = total.astype(BF)
        rest = total - high.astype(F32)
        middle = rest.astype(BF)
        last = (rest - middle.astype(F32)).astype(BF)
        w = w_ref[W12:WSUM]
        third = sum(lax.dot_general(part, w, MINOR, preferred_element_type=F32) for part in (last, middle, high))
        out_ref[...] = jnp.concatenate([a1[...], a2[...], third], axis=1)


def table_sums(hits, got, weights):
    total = hits.shape[2]
    depth = SOURCES * PD
    return pl.pallas_call(
        table_kernel,
        grid=(total // depth,),
        in_specs=[
            pl.BlockSpec((3, ROWS, depth), lambda i: (0, 0, i)),
            pl.BlockSpec((SOURCES, PD + W12, PD), lambda i: (i, 0, 0)),
            pl.BlockSpec((WSUM, PD), lambda i: (0, 0)),
        ],
        out_specs=pl.BlockSpec((ROWS, WSUM), lambda i: (0, 0)),
        out_shape=jax.ShapeDtypeStruct((ROWS, WSUM), F32),
        scratch_shapes=[
            pltpu.VMEM((ROWS, W1), F32),
            pltpu.VMEM((ROWS, W2), F32),
            pltpu.VMEM((ROWS, PD), F32),
        ],
        compiler_params=pltpu.CompilerParams(vmem_limit_bytes=40 * 2**20),
        cost_estimate=pl.CostEstimate(flops=7 * 10**9, bytes_accessed=57 * 10**6, transcendentals=0),
    )(hits, got, weights)


def positions(assign):
    slots = jnp.arange(SLOTS, dtype=jnp.int32)
    at = coords(slots // 8, slots % 8)
    rows = [slots]
    for order in ORDERS:
        rows.append(((at["core"] * 4 + at[order[0]]) * 4 + at[order[1]]) * 4 + at[order[2]])
    held = assign[None, :] == slots[:, None]
    return jnp.stack([jnp.sum(jnp.where(held, row[None, :], 0), axis=1) for row in rows])


def local(grad_out, pooled, proj, assign, indices, lengths):
    scale = 1.0 / math.sqrt(grad_out.shape[0] * SLOTS)
    axes = ("node", "local")
    w12 = lax.all_gather(proj[:, :W12], axes, tiled=True)
    pos = positions(assign)
    send, *bands = prepare(pos, grad_out, pooled, w12)
    got = lax.all_to_all(send, axes, split_axis=0, concat_axis=0, tiled=True)
    proj_grad = reduce_bands(bands, scale)
    hits = count_rows(jnp.transpose(indices[0], (1, 2, 0)), jnp.transpose(lengths[0], (1, 0)))
    table_grad = table_sums(hits, got, proj[0])
    return (table_grad[None], proj_grad[None])


def solution(mesh):
    placed = (
        P(("node", "local"), None, None),
        P(("node", "local"), None, None),
        P(("node", "local"), None, None),
        P(),
        P(("node", "local"), None, None, None),
        P(("node", "local"), None, None),
    )
    return jax.shard_map(
        local,
        mesh=mesh,
        in_specs=placed,
        out_specs=(P(("node", "local"), None, None), P(("node", "local"), None, None)),
        check_vma=False,
    )
```

```python
import functools
import math

import jax
import jax.numpy as jnp
from jax import lax
from jax.experimental import pallas as pl
from jax.experimental.pallas import tpu as pltpu
from jax.sharding import PartitionSpec as P

ROWS = 512
W1 = 16
W2 = 48
W3 = 192
W12 = W1 + W2
WSUM = W12 + W3
PD = 128
BAG = 8
SLOTS = 128
PER = 16
BANDS = ((0, 96), (96, 80), (176, 80))
ORDERS = (("z", "y", "x"), ("y", "x", "z"), ("x", "z", "y"))
BF = jnp.bfloat16
F32 = jnp.float32
MINOR = (((1,), (1,)), ((), ()))
MAJOR = (((0,), (0,)), ((), ()))


def coords(node, local):
    return {
        "core": node % 2,
        "y": node // 2 % 4,
        "x": local // 2,
        "z": local % 2 * 2 + node // 8,
    }


def place(at):
    return {
        "node": (at["z"] % 2 * 4 + at["y"]) * 2 + at["core"],
        "local": at["x"] * 2 + at["z"] // 2,
    }


def prepare_kernel(
    pos_ref, g_ref, q_ref, w_ref, send_ref, b0_ref, b1_ref, b2_ref, gt, qt, stage, pstage, ssem, psem, *, steps
):
    step = pl.program_id(0)
    now = lax.rem(step, 2)
    bands = (b0_ref, b1_ref, b2_ref)

    def drain(half):
        pltpu.make_async_copy(stage.at[half], stage.at[half], ssem.at[half]).wait()
        pltpu.make_async_copy(pstage.at[half], pstage.at[half], psem.at[half]).wait()

    @pl.when(step >= 2)
    def _():
        drain(now)

    gt[...] = jnp.swapaxes(g_ref[...], 0, 1)
    qt[...] = jnp.swapaxes(q_ref[...], 0, 1)

    def one(k, carry):
        group = step * PER + k
        slot = pos_ref[0, group]
        g = gt[k]
        q = qt[k]
        w = w_ref[pos_ref[1, group]]
        d1 = lax.dot_general(w[0:W1], g[:, 0:PD], MINOR, preferred_element_type=F32)
        d2 = lax.dot_general(w[W1:W12], g[:, PD : 2 * PD], MINOR, preferred_element_type=F32)
        stage[now, k, 0:PD] = g[:, 2 * PD : 3 * PD]
        stage[now, k, PD : PD + W1] = d1.astype(BF)
        stage[now, k, PD + W1 : PD + W12] = d2.astype(BF)
        third = lax.dot_general(q, g[:, 2 * PD : 3 * PD], MAJOR, preferred_element_type=F32)
        both = lax.dot_general(q[:, 0:W12], g[:, 0 : 2 * PD], MAJOR, preferred_element_type=F32)
        pstage[now, k, 0:W1] = both[0:W1, 0:PD]
        pstage[now, k, W1:W12] = both[W1:W12, PD : 2 * PD]
        pstage[now, k, W12:WSUM] = third[W12:WSUM]
        pltpu.make_async_copy(stage.at[now, k], send_ref.at[slot], ssem.at[now]).start()
        for n, (at, rows) in enumerate(BANDS):
            pltpu.make_async_copy(
                pstage.at[now, k, pl.ds(at, rows)], bands[n].at[pos_ref[2 + n, group]], psem.at[now]
            ).start()
        return carry

    lax.fori_loop(0, PER, one, 0, unroll=4)

    @pl.when(step == steps - 1)
    def _():
        drain(1 - now)
        drain(now)


def prepare(pos, grad_out, pooled, w12):
    count = grad_out.shape[0]
    steps = SLOTS // PER
    return pl.pallas_call(
        functools.partial(prepare_kernel, steps=steps),
        grid_spec=pltpu.PrefetchScalarGridSpec(
            num_scalar_prefetch=1,
            grid=(steps,),
            in_specs=[
                pl.BlockSpec((count, PER, 3 * PD), lambda i, p: (0, i, 0)),
                pl.BlockSpec((count, PER, WSUM), lambda i, p: (0, i, 0)),
                pl.BlockSpec((SLOTS, W12, PD), lambda i, p: (0, 0, 0)),
            ],
            out_specs=[pl.BlockSpec(memory_space=pl.ANY)] * 4,
            scratch_shapes=[
                pltpu.VMEM((PER, count, 3 * PD), BF),
                pltpu.VMEM((PER, count, WSUM), BF),
                pltpu.VMEM((2, PER, PD + W12, count), BF),
                pltpu.VMEM((2, PER, WSUM, PD), F32),
                pltpu.SemaphoreType.DMA((2,)),
                pltpu.SemaphoreType.DMA((2,)),
            ],
        ),
        out_shape=[jax.ShapeDtypeStruct((SLOTS, PD + W12, count), BF)]
        + [jax.ShapeDtypeStruct((SLOTS, rows, PD), F32) for _, rows in BANDS],
        compiler_params=pltpu.CompilerParams(vmem_limit_bytes=48 * 2**20),
        cost_estimate=pl.CostEstimate(flops=4 * 10**9, bytes_accessed=50 * 10**6, transcendentals=0),
    )(pos, grad_out, pooled, w12)


def reduce_kernel(scale, *refs):
    bands, out_ref = refs[0:3], refs[3]
    own, got, s1, r1, t, r2, u, r3 = (refs[4 + 3 * n : 7 + 3 * n] for n in range(8))
    own_sem, core_sem, sem1, sem2, sem3 = refs[28:33]
    me = coords(lax.axis_index("node"), lax.axis_index("local"))
    core = me["core"]

    def other(axis, hop):
        size = 2 if axis == "core" else 4
        return place(dict(me, **{axis: (me[axis] + hop) % size}))

    partners = [other("core", 1)] + [other(axis, hop) for axis in "xyz" for hop in (1, 2, 3)]
    barrier = pltpu.get_barrier_semaphore()
    for partner in partners:
        pl.semaphore_signal(barrier, inc=1, device_id=partner, device_id_type=pl.DeviceIdType.MESH)
    pl.semaphore_wait(barrier, len(partners))

    def send(src, dst, sems, at, to):
        copy = pltpu.make_async_remote_copy(
            src_ref=src,
            dst_ref=dst,
            send_sem=sems.at[(0,) + at],
            recv_sem=sems.at[(1,) + at],
            device_id=to,
            device_id_type=pl.DeviceIdType.MESH,
        )
        copy.start()
        return copy

    hops = (1, 2, 3, 0)
    loads, core_copies = {}, {}
    for hop in hops:
        for n in range(3):
            at = (me[ORDERS[n][0]] + hop) % 4 * 16
            loads[n, hop] = pltpu.make_async_copy(
                bands[n].at[pl.ds(core * 64 + at, 16)], own[n].at[hop], own_sem.at[n, hop]
            )
            loads[n, hop].start()
            core_copies[n, hop] = send(
                bands[n].at[pl.ds((1 - core) * 64 + at, 16)], got[n].at[hop], core_sem, (n, hop), other("core", 1)
            )

    first = {}
    for hop in hops:
        for n in range(3):
            loads[n, hop].wait()
            core_copies[n, hop].wait_recv()

            def add(i, carry):
                total = own[n][hop, i] + got[n][hop, i]
                if hop == 0:
                    t[n][i] = total
                else:
                    s1[n][hop - 1, i] = total.astype(BF)
                return carry

            lax.fori_loop(0, 16, add, 0)
            if hop:
                first[n, hop] = send(
                    s1[n].at[hop - 1], r1[n].at[hop - 1], sem1, (n, hop - 1), other(ORDERS[n][0], hop)
                )

    second = {}
    for n in range(3):
        for hop in (1, 2, 3):
            first[n, hop].wait_recv()

        def add(i, carry):
            t[n][i] = t[n][i] + (
                r1[n][0, i].astype(F32) + r1[n][1, i].astype(F32) + r1[n][2, i].astype(F32)
            )
            return carry

        lax.fori_loop(0, 16, add, 0)
        for hop in (1, 2, 3):
            at = (me[ORDERS[n][1]] + hop) % 4 * 4
            second[n, hop] = send(
                t[n].at[pl.ds(at, 4)], r2[n].at[hop - 1], sem2, (n, hop - 1), other(ORDERS[n][1], hop)
            )

    third = {}
    for n in range(3):
        for hop in (1, 2, 3):
            second[n, hop].wait_recv()
        at = me[ORDERS[n][1]] * 4

        def add(i, carry):
            u[n][i] = t[n][at + i] + (r2[n][0, i] + r2[n][1, i] + r2[n][2, i])
            return carry

        lax.fori_loop(0, 4, add, 0)
        for hop in (1, 2, 3):
            to = (me[ORDERS[n][2]] + hop) % 4
            third[n, hop] = send(u[n].at[to], r3[n].at[hop - 1], sem3, (n, hop - 1), other(ORDERS[n][2], hop))

    for n, (start, rows) in enumerate(BANDS):
        for hop in (1, 2, 3):
            third[n, hop].wait_recv()
        total = u[n][me[ORDERS[n][2]]] + (r3[n][0] + r3[n][1] + r3[n][2])
        out_ref[start : start + rows] = total * scale

    for copies in (core_copies, first, second, third):
        for copy in copies.values():
            copy.wait_send()


def reduce_bands(bands, scale):
    def each(*lead, kind=F32):
        return [pltpu.VMEM(lead + (rows, PD), kind) for _, rows in BANDS]

    return pl.pallas_call(
        functools.partial(reduce_kernel, scale),
        in_specs=[pl.BlockSpec(memory_space=pl.ANY)] * 3,
        out_specs=pl.BlockSpec(memory_space=pltpu.VMEM),
        out_shape=jax.ShapeDtypeStruct((WSUM, PD), F32),
        scratch_shapes=[
            *each(4, 16),
            *each(4, 16),
            *each(3, 16, kind=BF),
            *each(3, 16, kind=BF),
            *each(16),
            *each(3, 4),
            *each(4),
            *each(3),
            pltpu.SemaphoreType.DMA((3, 4)),
            pltpu.SemaphoreType.DMA((2, 3, 4)),
            pltpu.SemaphoreType.DMA((2, 3, 3)),
            pltpu.SemaphoreType.DMA((2, 3, 3)),
            pltpu.SemaphoreType.DMA((2, 3, 3)),
        ],
        compiler_params=pltpu.CompilerParams(
            collective_id=0, has_side_effects=True, vmem_limit_bytes=48 * 2**20
        ),
        cost_estimate=pl.CostEstimate(flops=10**7, bytes_accessed=40 * 10**6, transcendentals=0),
    )(*bands)


COLS = 512
PACK = 8
LOW = ROWS // PACK


def count_columns(idx_ref, len_ref, out_ref, first, columns):
    rows = lax.broadcasted_iota(jnp.int32, (LOW, 128), 0)
    order = lax.broadcasted_iota(jnp.int32, (BAG, 128), 0)

    def column(c, carry):
        at = pl.multiple_of(c * 128, 128)
        for table in range(3):
            idx = idx_ref[table, :, pl.ds(at, 128)]
            keep = order < len_ref[table : table + 1, pl.ds(at, 128)]
            low = idx & (LOW - 1)
            unit = jnp.where(keep, lax.shift_left(jnp.ones_like(idx), 4 * lax.shift_right_logical(idx, 6)), 0)
            total = jnp.zeros((LOW, 128), jnp.int32)
            for j in range(BAG):
                total = total + jnp.where(low[j : j + 1] == rows, unit[j : j + 1], 0)
            out_ref[table, :, pl.ds(at, 128)] = total
        return carry

    lax.fori_loop(first, first + columns, column, 0)


SHARES = (24, 32, 56, 16)


def gather_kernel(w_ref, idx_ref, len_ref, all_ref, counts_ref, held, counts, own_sem, sems, core_sems, out_sems):
    me = coords(lax.axis_index("node"), lax.axis_index("local"))
    core, z, y, x = me["core"], me["z"], me["y"], me["x"]

    def other(axis, hop):
        size = 2 if axis == "core" else 4
        return place(dict(me, **{axis: (me[axis] + hop) % size}))

    own = pltpu.make_async_copy(w_ref, held.at[core, z, y, x], own_sem)
    own.start()
    partners = [other("core", 1)] + [other(axis, hop) for axis in "xyz" for hop in (1, 2, 3)]
    barrier = pltpu.get_barrier_semaphore()
    for partner in partners:
        pl.semaphore_signal(barrier, inc=1, device_id=partner, device_id_type=pl.DeviceIdType.MESH)
    pl.semaphore_wait(barrier, len(partners))
    own.wait()

    stages = (("x", held.at[core, z, y, x]), ("y", held.at[core, z, y]), ("z", held.at[core, z]))
    copies = []
    first = 0
    writes = []

    def work(stage):
        nonlocal first
        columns = SHARES[stage]
        count_columns(idx_ref, len_ref, counts, first, columns)
        span = pl.ds(first * 128, columns * 128)
        write = pltpu.make_async_copy(counts.at[:, :, span], counts_ref.at[:, :, span], out_sems.at[stage])
        write.start()
        writes.append(write)
        first += columns

    def send(block, to, send_sem, recv_sem):
        copy = pltpu.make_async_remote_copy(
            src_ref=block,
            dst_ref=block,
            send_sem=send_sem,
            recv_sem=recv_sem,
            device_id=to,
            device_id_type=pl.DeviceIdType.MESH,
        )
        copy.start()
        copies.append(copy)
        return copy

    for stage, (axis, block) in enumerate(stages):
        sent = [
            send(block, other(axis, hop), sems.at[0, stage, hop - 1], sems.at[1, stage, hop - 1]) for hop in (1, 2, 3)
        ]
        work(stage)
        for copy in sent:
            copy.wait_recv()
    last = send(held.at[core], other("core", 1), core_sems.at[0], core_sems.at[1])
    work(3)
    last.wait_recv()
    whole = pltpu.make_async_copy(held, all_ref, own_sem)
    whole.start()
    for copy in copies:
        copy.wait_send()
    whole.wait()
    for write in writes:
        write.wait()


def gather_and_count(w12, lookups, lengths):
    total = lookups.shape[2]
    return pl.pallas_call(
        gather_kernel,
        in_specs=[pl.BlockSpec(memory_space=pltpu.VMEM)] * 3,
        out_specs=[pl.BlockSpec(memory_space=pl.ANY)] * 2,
        out_shape=[
            jax.ShapeDtypeStruct((2, 4, 4, 4, W12, PD), BF),
            jax.ShapeDtypeStruct((3, LOW, total), jnp.int32),
        ],
        scratch_shapes=[
            pltpu.VMEM((2, 4, 4, 4, W12, PD), BF),
            pltpu.VMEM((3, LOW, total), jnp.int32),
            pltpu.SemaphoreType.DMA,
            pltpu.SemaphoreType.DMA((2, 3, 3)),
            pltpu.SemaphoreType.DMA((2,)),
            pltpu.SemaphoreType.DMA((4,)),
        ],
        compiler_params=pltpu.CompilerParams(
            collective_id=1, has_side_effects=True, vmem_limit_bytes=32 * 2**20
        ),
        cost_estimate=pl.CostEstimate(flops=10**9, bytes_accessed=20 * 10**6, transcendentals=0),
    )(w12, lookups, lengths)


SOURCES = 16


def table_kernel(counts_ref, got_ref, w_ref, out_ref, a1, a2, a3):
    step = pl.program_id(0)

    @pl.when(step == 0)
    def _():
        a1[...] = jnp.zeros_like(a1)
        a2[...] = jnp.zeros_like(a2)
        a3[...] = jnp.zeros_like(a3)

    def hits(table):
        words = counts_ref[table]
        return jnp.concatenate(
            [(lax.shift_right_logical(words, 4 * part) & 15).astype(F32).astype(BF) for part in range(PACK)], axis=0
        )

    wide = got_ref[:, 0:PD, :].reshape(SOURCES * PD, PD)
    narrow = jnp.concatenate([got_ref[s, PD : PD + W12, :] for s in range(SOURCES)], axis=1)
    a1[...] += lax.dot_general(hits(0), narrow[0:W1], MINOR, preferred_element_type=F32)
    a2[...] += lax.dot_general(hits(1), narrow[W1:W12], MINOR, preferred_element_type=F32)
    a3[...] += jnp.dot(hits(2), wide, preferred_element_type=F32)

    @pl.when(step == pl.num_programs(0) - 1)
    def _():
        total = a3[...]
        high = total.astype(BF)
        rest = total - high.astype(F32)
        middle = rest.astype(BF)
        last = (rest - middle.astype(F32)).astype(BF)
        w = w_ref[W12:WSUM]
        third = sum(lax.dot_general(part, w, MINOR, preferred_element_type=F32) for part in (last, middle, high))
        out_ref[...] = jnp.concatenate([a1[...], a2[...], third], axis=1)


def table_sums(counts, got, weights):
    total = counts.shape[2]
    depth = SOURCES * PD
    return pl.pallas_call(
        table_kernel,
        grid=(total // depth,),
        in_specs=[
            pl.BlockSpec((3, LOW, depth), lambda i: (0, 0, i)),
            pl.BlockSpec((SOURCES, PD + W12, PD), lambda i: (i, 0, 0)),
            pl.BlockSpec((WSUM, PD), lambda i: (0, 0)),
        ],
        out_specs=pl.BlockSpec((ROWS, WSUM), lambda i: (0, 0)),
        out_shape=jax.ShapeDtypeStruct((ROWS, WSUM), F32),
        scratch_shapes=[
            pltpu.VMEM((ROWS, W1), F32),
            pltpu.VMEM((ROWS, W2), F32),
            pltpu.VMEM((ROWS, PD), F32),
        ],
        compiler_params=pltpu.CompilerParams(vmem_limit_bytes=40 * 2**20),
        cost_estimate=pl.CostEstimate(flops=7 * 10**9, bytes_accessed=20 * 10**6, transcendentals=0),
    )(counts, got, weights)


def positions(assign):
    slots = jnp.arange(SLOTS, dtype=jnp.int32)
    at = coords(slots // 8, slots % 8)
    rows = [slots, ((at["core"] * 4 + at["z"]) * 4 + at["y"]) * 4 + at["x"]]
    for order in ORDERS:
        rows.append(((at["core"] * 4 + at[order[0]]) * 4 + at[order[1]]) * 4 + at[order[2]])
    held = assign[None, :] == slots[:, None]
    return jnp.stack([jnp.sum(jnp.where(held, row[None, :], 0), axis=1) for row in rows])


def local(grad_out, pooled, proj, assign, indices, lengths):
    scale = 1.0 / math.sqrt(grad_out.shape[0] * SLOTS)
    axes = ("node", "local")
    pos = positions(assign)
    lookups = jnp.transpose(indices[0], (1, 2, 0))
    w12, counts = gather_and_count(proj[0, :W12], lookups, jnp.transpose(lengths[0], (1, 0)))
    send, *bands = prepare(pos, grad_out, pooled, w12.reshape(SLOTS, W12, PD))
    got = lax.all_to_all(send, axes, split_axis=0, concat_axis=0, tiled=True)
    proj_grad = reduce_bands(bands, scale)
    table_grad = table_sums(counts, got, proj[0])
    return (table_grad[None], proj_grad[None])


def solution(mesh):
    placed = (
        P(("node", "local"), None, None),
        P(("node", "local"), None, None),
        P(("node", "local"), None, None),
        P(),
        P(("node", "local"), None, None, None),
        P(("node", "local"), None, None),
    )
    return jax.shard_map(
        local,
        mesh=mesh,
        in_specs=placed,
        out_specs=(P(("node", "local"), None, None), P(("node", "local"), None, None)),
        check_vma=False,
    )
```

```python
import functools
import math

import jax
import jax.numpy as jnp
from jax import lax
from jax.experimental import pallas as pl
from jax.experimental.pallas import tpu as pltpu
from jax.sharding import PartitionSpec as P

ROWS = 512
W1 = 16
W2 = 48
W3 = 192
W12 = W1 + W2
WSUM = W12 + W3
PD = 128
BAG = 8
SLOTS = 128
PER = 16
BANDS = ((0, 96), (96, 80), (176, 80))
ORDERS = (("z", "y", "x"), ("y", "x", "z"), ("x", "z", "y"))
BF = jnp.bfloat16
F32 = jnp.float32
MINOR = (((1,), (1,)), ((), ()))
MAJOR = (((0,), (0,)), ((), ()))


def coords(node, local):
    return {
        "core": node % 2,
        "y": node // 2 % 4,
        "x": local // 2,
        "z": local % 2 * 2 + node // 8,
    }


def place(at):
    return {
        "node": (at["z"] % 2 * 4 + at["y"]) * 2 + at["core"],
        "local": at["x"] * 2 + at["z"] // 2,
    }


LANES = ((0, 16), (16, 16), (32, 32))
CHUNKS = SLOTS // PER
GROUP = 8


def prepare_kernel(
    assign_ref, w_ref, g_ref, q_ref, send_ref, b0_ref, b1_ref, b2_ref,
    held0, held1, held2, gbuf, qbuf, gt, qt, stage, pstage,
    own_sem, hop_sem, core_sem, gsem, qsem, ssem, psem,
):
    me = coords(lax.axis_index("node"), lax.axis_index("local"))
    bands = (b0_ref, b1_ref, b2_ref)
    held = (held0, held1, held2)

    def other(axis, hop):
        size = 2 if axis == "core" else 4
        return place(dict(me, **{axis: (me[axis] + hop) % size}))

    def load(chunk):
        rows = pl.ds(pl.multiple_of(chunk * PER, PER), PER)
        half = lax.rem(chunk, 2)
        return (
            pltpu.make_async_copy(g_ref.at[:, rows], gbuf.at[half], gsem.at[half]),
            pltpu.make_async_copy(q_ref.at[:, rows], qbuf.at[half], qsem.at[half]),
        )

    for chunk in range(2):
        for copy in load(jnp.int32(chunk)):
            copy.start()

    own = []
    for n, (start, rows) in enumerate(LANES):
        a, b, c = (me[axis] for axis in ORDERS[n])
        own.append(
            pltpu.make_async_copy(w_ref.at[pl.ds(start, rows)], held[n].at[me["core"], a, b, c], own_sem.at[n])
        )
        own[n].start()

    partners = [other("core", 1)] + [other(axis, hop) for axis in "xyz" for hop in (1, 2, 3)]
    barrier = pltpu.get_barrier_semaphore()
    for partner in partners:
        pl.semaphore_signal(barrier, inc=1, device_id=partner, device_id_type=pl.DeviceIdType.MESH)
    for copy in own:
        copy.wait()

    copies = []

    def send(block, to, sems, where):
        copy = pltpu.make_async_remote_copy(
            src_ref=block,
            dst_ref=block,
            send_sem=sems.at[(0,) + where],
            recv_sem=sems.at[(1,) + where],
            device_id=to,
            device_id_type=pl.DeviceIdType.MESH,
        )
        copy.start()
        copies.append(copy)
        return copy

    def spread(turn):
        sent = []
        for n in range(3):
            a, b, c = (me[axis] for axis in ORDERS[n])
            block = held[n].at[(me["core"], a, b, c)[: 4 - turn]]
            axis = ORDERS[n][2 - turn]
            sent += [send(block, other(axis, hop), hop_sem, (n, turn, hop - 1)) for hop in (1, 2, 3)]
        return sent

    def arrive(sent):
        for copy in sent:
            copy.wait_recv()

    def turn_over(first, last):
        def one(chunk, carry):
            half = lax.rem(chunk, 2)
            for copy in load(chunk):
                copy.wait()
            rows = pl.ds(pl.multiple_of(chunk * PER, PER), PER)
            gt[rows] = jnp.swapaxes(gbuf[half], 0, 1)
            qt[rows] = jnp.swapaxes(qbuf[half], 0, 1)

            @pl.when(chunk + 2 < CHUNKS)
            def _():
                for copy in load(chunk + 2):
                    copy.start()

            return carry

        lax.fori_loop(first, last, one, 0)

    def drain(buffer, sems, half):
        pltpu.make_async_copy(buffer.at[half], buffer.at[half], sems.at[half]).wait()

    def partial_sums(first, last):
        def some(batch, carry):
            now = lax.rem(batch, 2)
            core, y, z_low = batch % 2, batch // 2 % 4, batch // 8

            @pl.when(batch >= 2)
            def _():
                drain(pstage, psem, now)

            for k in range(GROUP):
                to = {"core": core, "y": y, "x": k // 2, "z": k % 2 * 2 + z_low}
                group = assign_ref[batch * GROUP + k]
                g = gt[group]
                q = qt[group]
                wide = lax.dot_general(q, g[:, 2 * PD : 3 * PD], MAJOR, preferred_element_type=F32)
                both = lax.dot_general(q[:, 0:W12], g[:, 0 : 2 * PD], MAJOR, preferred_element_type=F32)
                pstage[now, k, 0:W1] = both[0:W1, 0:PD]
                pstage[now, k, W1:W12] = both[W1:W12, PD : 2 * PD]
                pstage[now, k, W12:WSUM] = wide[W12:WSUM]
            for k in range(GROUP):
                to = {"core": core, "y": y, "x": k // 2, "z": k % 2 * 2 + z_low}
                for n, (start, rows) in enumerate(BANDS):
                    a, b, c = (to[axis] for axis in ORDERS[n])
                    pltpu.make_async_copy(
                        pstage.at[now, k, pl.ds(start, rows)],
                        bands[n].at[((core * 4 + a) * 4 + b) * 4 + c],
                        psem.at[now],
                    ).start()
            return carry

        lax.fori_loop(first, last, some, 0)

    def exchange_rows(core, first):
        def some(turn, carry):
            now = lax.rem(turn, 2)
            batch = turn * 2 + core
            y, z_low = turn % 4, turn // 4

            @pl.when(first + turn >= 2)
            def _():
                drain(stage, ssem, now)

            for k in range(GROUP):
                to = {"y": y, "x": k // 2, "z": k % 2 * 2 + z_low}
                g = gt[assign_ref[batch * GROUP + k]]
                w = [held[n][(core,) + tuple(to[axis] for axis in ORDERS[n])] for n in range(3)]
                none = jnp.zeros((W1, PD), BF)
                w = jnp.concatenate(
                    [
                        jnp.concatenate([w[0], none], axis=1),
                        jnp.concatenate([none, w[1]], axis=1),
                        jnp.concatenate([jnp.concatenate([none, none], axis=0), w[2]], axis=1),
                    ],
                    axis=0,
                )
                at = k % 2 * 4 + k // 2
                stage[now, at, 0:PD] = g[:, 2 * PD : 3 * PD]
                stage[now, at, PD : PD + W12] = lax.dot_general(
                    w, g[:, 0 : 2 * PD], MINOR, preferred_element_type=F32
                ).astype(BF)
            for high in range(2):
                pltpu.make_async_copy(
                    stage.at[now, pl.ds(high * 4, 4)], send_ref.at[high * 2 + z_low, y, core], ssem.at[now]
                ).start()
            return carry

        lax.fori_loop(0, SLOTS // GROUP // 2, some, 0)

    batches = SLOTS // GROUP
    turn_over(0, 3)
    pl.semaphore_wait(barrier, len(partners))
    sent = spread(0)
    turn_over(3, 6)
    arrive(sent)
    sent = spread(1)
    turn_over(6, CHUNKS)
    partial_sums(0, 4)
    arrive(sent)
    sent = spread(2)
    partial_sums(4, batches)
    arrive(sent)
    sent = [send(held[n].at[me["core"]], other("core", 1), core_sem, (n,)) for n in range(3)]
    exchange_rows(me["core"], 0)
    arrive(sent)
    exchange_rows(1 - me["core"], 2)
    for half in range(2):
        drain(pstage, psem, half)
        drain(stage, ssem, half)
    for copy in copies:
        copy.wait_send()


def prepare(assign, w12, grad_out, pooled):
    count = grad_out.shape[0]
    return pl.pallas_call(
        prepare_kernel,
        in_specs=[
            pl.BlockSpec(memory_space=pltpu.SMEM),
            pl.BlockSpec(memory_space=pltpu.VMEM),
            pl.BlockSpec(memory_space=pl.ANY),
            pl.BlockSpec(memory_space=pl.ANY),
        ],
        out_specs=[pl.BlockSpec(memory_space=pl.ANY)] * 4,
        out_shape=[jax.ShapeDtypeStruct((4, 4, 2, 4, PD + W12, count), BF)]
        + [jax.ShapeDtypeStruct((SLOTS, rows, PD), F32) for _, rows in BANDS],
        scratch_shapes=[pltpu.VMEM((2, 4, 4, 4, rows, PD), BF) for _, rows in LANES]
        + [
            pltpu.VMEM((2, count, PER, 3 * PD), BF),
            pltpu.VMEM((2, count, PER, WSUM), BF),
            pltpu.VMEM((SLOTS, count, 3 * PD), BF),
            pltpu.VMEM((SLOTS, count, WSUM), BF),
            pltpu.VMEM((2, GROUP, PD + W12, count), BF),
            pltpu.VMEM((2, GROUP, WSUM, PD), F32),
            pltpu.SemaphoreType.DMA((3,)),
            pltpu.SemaphoreType.DMA((2, 3, 3, 3)),
            pltpu.SemaphoreType.DMA((2, 3)),
            pltpu.SemaphoreType.DMA((2,)),
            pltpu.SemaphoreType.DMA((2,)),
            pltpu.SemaphoreType.DMA((2,)),
            pltpu.SemaphoreType.DMA((2,)),
        ],
        compiler_params=pltpu.CompilerParams(
            collective_id=1, has_side_effects=True, vmem_limit_bytes=48 * 2**20
        ),
        cost_estimate=pl.CostEstimate(flops=4 * 10**9, bytes_accessed=50 * 10**6, transcendentals=0),
    )(assign, w12, grad_out, pooled)


PACK = 8
LOW = ROWS // PACK


def count_columns(idx_ref, len_ref, out_ref, first, columns):
    rows = lax.broadcasted_iota(jnp.int32, (LOW, 128), 0)
    order = lax.broadcasted_iota(jnp.int32, (BAG, 128), 0)

    def column(c, carry):
        at = pl.multiple_of(c * 128, 128)
        for table in range(3):
            idx = idx_ref[table, :, pl.ds(at, 128)]
            keep = order < len_ref[table : table + 1, pl.ds(at, 128)]
            low = idx & (LOW - 1)
            unit = jnp.where(keep, lax.shift_left(jnp.ones_like(idx), 4 * lax.shift_right_logical(idx, 6)), 0)
            total = jnp.zeros((LOW, 128), jnp.int32)
            for j in range(BAG):
                total = total + jnp.where(low[j : j + 1] == rows, unit[j : j + 1], 0)
            out_ref[table, :, pl.ds(at, 128)] = total
        return carry

    lax.fori_loop(first, first + columns, column, 0)


SHARES = (40, 48, 40)
NEAR = (2, 0)
FAR = (1, 3)
NEAR_TURNS = ((0, 1), (1, 3), (0, 3), (1, 1), (0, 2), (1, 2), (0, 0), (1, 0))
FAR_TURNS = ((0, 1), (1, 3), (1, 1), (0, 3), (0, 2), (1, 2), (0, 0), (1, 0))


def exchange_kernel(scale, *refs):
    send_ref, bands, (idx_ref, len_ref, w_ref) = refs[0], refs[1:4], refs[4:7]
    table_ref, proj_ref = refs[7:9]
    own, got, s1, r1, t, r2, u, r3 = (refs[9 + 3 * n : 12 + 3 * n] for n in range(8))
    counts, near, far, here, a1, a2, a3 = refs[33:40]
    own_sem, core_sem, sem1, sem2, sem3, local_sem, near1, near2, far1, far2 = refs[40:50]
    me = coords(lax.axis_index("node"), lax.axis_index("local"))
    core, x, y, z = me["core"], me["x"], me["y"], me["z"]
    mine = core * 4 + x

    def other(**hops):
        at = dict(me)
        for axis, hop in hops.items():
            at[axis] = (me[axis] + hop) % (2 if axis == "core" else 4)
        return at

    row = [(c, m) for c in range(2) for m in (1, 3, 2, 0) if c or m]
    plane = [(n // 4, n % 4) for n in range(1, 16)]
    partners = [other(core=c, x=n) for c, n in row] + [other(z=n, y=m) for n, m in plane]
    barrier = pltpu.get_barrier_semaphore()
    for partner in partners:
        pl.semaphore_signal(barrier, inc=1, device_id=place(partner), device_id_type=pl.DeviceIdType.MESH)
    pl.semaphore_wait(barrier, len(partners))

    remote = []

    def send(src, dst, sems, at, to):
        copy = pltpu.make_async_remote_copy(
            src_ref=src,
            dst_ref=dst,
            send_sem=sems.at[(0,) + at],
            recv_sem=sems.at[(1,) + at],
            device_id=place(to),
            device_id_type=pl.DeviceIdType.MESH,
        )
        copy.start()
        remote.append(copy)
        return copy

    def keep(src, dst, n):
        copy = pltpu.make_async_copy(src, dst, local_sem.at[n])
        copy.start()
        return copy

    def arrive(sent, kept=()):
        for copy in sent:
            copy.wait_recv()
        for copy in kept:
            copy.wait()

    def near_first():
        sent, kept = [], []
        for c, m in row:
            to = other(core=c, x=m)
            for n in range(2):
                src = send_ref.at[(z + NEAR[n]) % 4, :, to["core"], to["x"]]
                sent.append(send(src, near.at[n, :, mine], near1, (n, c * 4 + m), to))
        for n in range(2):
            kept.append(keep(send_ref.at[(z + NEAR[n]) % 4, :, core, x], near.at[n, :, mine], n))
        return sent, kept

    def near_second():
        sent = {}
        for n, m in NEAR_TURNS:
            away = NEAR[n]
            to = other(z=away, y=m)
            if away or m:
                sent[n, m] = send(near.at[n, to["y"]], here.at[away, m], near2, (n, m), to)
        return sent, keep(near.at[1, y], here.at[0, 0], 2)

    def far_first():
        sent = []
        for n, m in FAR_TURNS:
            to = other(z=FAR[n], y=m)
            sent.append(send(send_ref.at[to["z"], to["y"]], far.at[n, m], far1, (n, m), to))
        return sent

    def far_second():
        sent, kept = {}, []
        for c, m in row:
            to = other(core=c, x=m)
            for n in range(2):
                src = far.at[n, :, to["core"], to["x"]]
                sent[n, c, m] = send(src, here.at[FAR[n], :, mine], far2, (n, c * 4 + m), to)
        for n in range(2):
            kept.append(keep(far.at[n, :, core, x], here.at[FAR[n], :, mine], 3 + n))
        return sent, kept

    def count(share):
        count_columns(idx_ref, len_ref, counts, sum(SHARES[:share]), SHARES[share])

    a1[...] = jnp.zeros_like(a1)
    a2[...] = jnp.zeros_like(a2)
    a3[...] = jnp.zeros_like(a3)

    def match(blocks, slots):
        def hits(table):
            words = jnp.concatenate(
                [counts[table, :, pl.ds(pl.multiple_of(slot * 128, 128), 128)] for slot in slots], axis=1
            )
            return jnp.concatenate(
                [(lax.shift_right_logical(words, 4 * part) & 15).astype(F32).astype(BF) for part in range(PACK)],
                axis=0,
            )

        wide = jnp.concatenate([block[0:PD] for block in blocks], axis=0)
        narrow = jnp.concatenate([block[PD : PD + W12] for block in blocks], axis=1)
        a1[...] += lax.dot_general(hits(0), narrow[0:W1], MINOR, preferred_element_type=F32)
        a2[...] += lax.dot_general(hits(1), narrow[W1:W12], MINOR, preferred_element_type=F32)
        a3[...] += jnp.dot(hits(2), wide, preferred_element_type=F32)

    def match_near(n, m):
        from_y, from_z = (y + 4 - m) % 4, (z + 4 - NEAR[n]) % 4
        first = (from_z % 2 * 4 + from_y) * 16 + from_z // 2
        match([here[NEAR[n], m, c * 4 + k] for c in range(2) for k in range(4)],
              [first + c * 8 + k * 2 for c in range(2) for k in range(4)])

    def match_far(n, c):
        from_core, from_z = (core + c) % 2, (z + 4 - FAR[n]) % 4

        def one(pair, carry):
            blocks, slots = [], []
            for i in range(2):
                m = pair * 2 + i
                from_y = (y + 4 - m) % 4
                first = ((from_z % 2 * 4 + from_y) * 2 + from_core) * 8 + from_z // 2
                for k in range(4):
                    blocks.append(here[FAR[n], m, from_core * 4 + k])
                    slots.append(first + k * 2)
            match(blocks, slots)
            return carry

        lax.fori_loop(0, 2, one, 0)

    near_one = near_first()
    far_one = far_first()
    hops = (1, 3, 2, 0)
    loads, core_copies = {}, {}
    for hop in hops:
        for n in range(3):
            at = (me[ORDERS[n][0]] + hop) % 4 * 16
            loads[n, hop] = pltpu.make_async_copy(
                bands[n].at[pl.ds(core * 64 + at, 16)], own[n].at[hop], own_sem.at[n, hop]
            )
            loads[n, hop].start()
            core_copies[n, hop] = send(
                bands[n].at[pl.ds((1 - core) * 64 + at, 16)], got[n].at[hop], core_sem, (n, hop), other(core=1)
            )
    count(0)

    first = {}
    for hop in hops:
        for n in range(3):
            loads[n, hop].wait()
            core_copies[n, hop].wait_recv()

            def add(i, carry):
                total = own[n][hop, i] + got[n][hop, i]
                if hop == 0:
                    t[n][i] = total
                else:
                    s1[n][hop - 1, i] = total.astype(BF)
                return carry

            lax.fori_loop(0, 16, add, 0)
            if hop:
                first[n, hop] = send(
                    s1[n].at[hop - 1], r1[n].at[hop - 1], sem1, (n, hop - 1), other(**{ORDERS[n][0]: hop})
                )

    count(1)
    arrive(*near_one)
    near_two, near_kept = near_second()
    arrive(far_one)
    far_two, far_kept = far_second()

    second = {}
    for n in range(3):
        arrive([first[n, hop] for hop in (1, 2, 3)])

        def add(i, carry):
            t[n][i] = t[n][i] + (
                r1[n][0, i].astype(F32) + r1[n][1, i].astype(F32) + r1[n][2, i].astype(F32)
            )
            return carry

        lax.fori_loop(0, 16, add, 0)
        for hop in (1, 2, 3):
            at = (me[ORDERS[n][1]] + hop) % 4 * 4
            second[n, hop] = send(
                t[n].at[pl.ds(at, 4)], r2[n].at[hop - 1], sem2, (n, hop - 1), other(**{ORDERS[n][1]: hop})
            )

    count(2)

    third = {}
    for n in range(3):
        arrive([second[n, hop] for hop in (1, 2, 3)])
        at = me[ORDERS[n][1]] * 4

        def add(i, carry):
            u[n][i] = t[n][at + i] + (r2[n][0, i] + r2[n][1, i] + r2[n][2, i])
            return carry

        lax.fori_loop(0, 4, add, 0)
        for hop in (1, 2, 3):
            to = (me[ORDERS[n][2]] + hop) % 4
            third[n, hop] = send(u[n].at[to], r3[n].at[hop - 1], sem3, (n, hop - 1), other(**{ORDERS[n][2]: hop}))

    near_kept.wait()
    match_near(1, 0)
    for n, m in NEAR_TURNS[:4]:
        near_two[n, m].wait_recv()
        match_near(n, m)
    for n in range(2):
        arrive([far_two[n, 0, m] for m in (1, 3, 2)], [far_kept[n]])
        match_far(n, 0)
    for n, (start, rows) in enumerate(BANDS):
        arrive([third[n, hop] for hop in (1, 2, 3)])
        total = u[n][me[ORDERS[n][2]]] + (r3[n][0] + r3[n][1] + r3[n][2])
        proj_ref[start : start + rows] = total * scale
    for n, m in NEAR_TURNS[4:7]:
        near_two[n, m].wait_recv()
        match_near(n, m)
    for n in range(2):
        arrive([far_two[n, 1, m] for m in range(4)])
        match_far(n, 1)

    total = a3[...]
    high = total.astype(BF)
    rest = total - high.astype(F32)
    middle = rest.astype(BF)
    last = (rest - middle.astype(F32)).astype(BF)
    w = w_ref[W12:WSUM]
    widest = sum(lax.dot_general(part, w, MINOR, preferred_element_type=F32) for part in (last, middle, high))
    table_ref[...] = jnp.concatenate([a1[...], a2[...], widest], axis=1)
    for copy in remote:
        copy.wait_send()


def exchange(send, bands, lookups, lengths, weights, scale):
    total = lookups.shape[2]

    def each(*lead, kind=F32):
        return [pltpu.VMEM(lead + (rows, PD), kind) for _, rows in BANDS]

    block = (PD + W12, send.shape[-1])
    return pl.pallas_call(
        functools.partial(exchange_kernel, scale),
        in_specs=[pl.BlockSpec(memory_space=pl.ANY)] * 4 + [pl.BlockSpec(memory_space=pltpu.VMEM)] * 3,
        out_specs=[pl.BlockSpec(memory_space=pltpu.VMEM)] * 2,
        out_shape=[
            jax.ShapeDtypeStruct((ROWS, WSUM), F32),
            jax.ShapeDtypeStruct((WSUM, PD), F32),
        ],
        scratch_shapes=[
            *each(4, 16),
            *each(4, 16),
            *each(3, 16, kind=BF),
            *each(3, 16, kind=BF),
            *each(16),
            *each(3, 4),
            *each(4),
            *each(3),
            pltpu.VMEM((3, LOW, total), jnp.int32),
            pltpu.VMEM((2, 4, 8) + block, BF),
            pltpu.VMEM((2, 4, 2, 4) + block, BF),
            pltpu.VMEM((4, 4, 8) + block, BF),
            pltpu.VMEM((ROWS, W1), F32),
            pltpu.VMEM((ROWS, W2), F32),
            pltpu.VMEM((ROWS, PD), F32),
            pltpu.SemaphoreType.DMA((3, 4)),
            pltpu.SemaphoreType.DMA((2, 3, 4)),
            pltpu.SemaphoreType.DMA((2, 3, 3)),
            pltpu.SemaphoreType.DMA((2, 3, 3)),
            pltpu.SemaphoreType.DMA((2, 3, 3)),
            pltpu.SemaphoreType.DMA((5,)),
            pltpu.SemaphoreType.DMA((2, 2, 8)),
            pltpu.SemaphoreType.DMA((2, 2, 4)),
            pltpu.SemaphoreType.DMA((2, 2, 4)),
            pltpu.SemaphoreType.DMA((2, 2, 8)),
        ],
        compiler_params=pltpu.CompilerParams(
            collective_id=0, has_side_effects=True, vmem_limit_bytes=62 * 2**20
        ),
        cost_estimate=pl.CostEstimate(flops=10**10, bytes_accessed=60 * 10**6, transcendentals=0),
    )(send, *bands, lookups, lengths, weights)


def local(grad_out, pooled, proj, assign, indices, lengths):
    scale = 1.0 / math.sqrt(grad_out.shape[0] * SLOTS)
    send, *bands = prepare(assign, proj[0, :W12], grad_out, pooled)
    lookups = jnp.transpose(indices[0], (1, 2, 0))
    table_grad, proj_grad = exchange(send, bands, lookups, jnp.transpose(lengths[0], (1, 0)), proj[0], scale)
    return (table_grad[None], proj_grad[None])


def solution(mesh):
    placed = (
        P(("node", "local"), None, None),
        P(("node", "local"), None, None),
        P(("node", "local"), None, None),
        P(),
        P(("node", "local"), None, None, None),
        P(("node", "local"), None, None),
    )
    return jax.shard_map(
        local,
        mesh=mesh,
        in_specs=placed,
        out_specs=(P(("node", "local"), None, None), P(("node", "local"), None, None)),
        check_vma=False,
    )
```

```python
import functools
import math

import jax
import jax.numpy as jnp
from jax import lax
from jax.experimental import pallas as pl
from jax.experimental.pallas import tpu as pltpu
from jax.sharding import PartitionSpec as P

ROWS = 512
W1 = 16
W2 = 48
W3 = 192
W12 = W1 + W2
WSUM = W12 + W3
PD = 128
BAG = 8
SLOTS = 128
PER = 16
BANDS = ((0, 96), (96, 80), (176, 80))
ORDERS = (("z", "y", "x"), ("y", "x", "z"), ("x", "z", "y"))
BF = jnp.bfloat16
F32 = jnp.float32
MINOR = (((1,), (1,)), ((), ()))
MAJOR = (((0,), (0,)), ((), ()))


def coords(node, local):
    return {
        "core": node % 2,
        "y": node // 2 % 4,
        "x": local // 2,
        "z": local % 2 * 2 + node // 8,
    }


def place(at):
    return {
        "node": (at["z"] % 2 * 4 + at["y"]) * 2 + at["core"],
        "local": at["x"] * 2 + at["z"] // 2,
    }


NEAR = (2, 0)
FAR = (1, 3)
NEAR_TURNS = ((0, 1), (1, 3), (0, 3), (1, 1), (0, 2), (1, 2), (0, 0), (1, 0))
FAR_TURNS = ((0, 1), (1, 3), (1, 1), (0, 3), (0, 2), (1, 2), (0, 0), (1, 0))
ROW = tuple((c, m) for c in range(2) for m in (1, 3, 2, 0) if c or m)


def neighbour(me, **hops):
    at = dict(me)
    for axis, hop in hops.items():
        at[axis] = (me[axis] + hop) % (2 if axis == "core" else 4)
    return at


def greet(me):
    partners = [neighbour(me, core=c, x=m) for c, m in ROW]
    partners += [neighbour(me, z=n // 4, y=n % 4) for n in range(1, 16)]
    barrier = pltpu.get_barrier_semaphore()
    for partner in partners:
        pl.semaphore_signal(barrier, inc=1, device_id=place(partner), device_id_type=pl.DeviceIdType.MESH)
    return lambda: pl.semaphore_wait(barrier, len(partners))


def sender(remote):
    def send(src, dst, sems, at, to):
        copy = pltpu.make_async_remote_copy(
            src_ref=src,
            dst_ref=dst,
            send_sem=sems.at[(0,) + at],
            recv_sem=sems.at[(1,) + at],
            device_id=place(to),
            device_id_type=pl.DeviceIdType.MESH,
        )
        copy.start()
        remote.append(copy)
        return copy

    return send


def keep(src, dst, sem):
    copy = pltpu.make_async_copy(src, dst, sem)
    copy.start()
    return copy


def arrive(sent, kept=()):
    for copy in sent:
        copy.wait_recv()
    for copy in kept:
        copy.wait()


def near_first(me, send, blocks, near, sems, own_sems):
    core, x, z = me["core"], me["x"], me["z"]
    mine = core * 4 + x
    sent = []
    for c, m in ROW:
        to = neighbour(me, core=c, x=m)
        for n in range(2):
            src = blocks.at[(z + NEAR[n]) % 4, :, to["core"], to["x"]]
            sent.append(send(src, near.at[n, :, mine], sems, (n, c * 4 + m), to))
    kept = [
        keep(blocks.at[(z + NEAR[n]) % 4, :, core, x], near.at[n, :, mine], own_sems.at[n]) for n in range(2)
    ]
    return sent, kept


def near_second(me, send, near, here, sems, own_sem):
    sent = {}
    for n, m in NEAR_TURNS:
        to = neighbour(me, z=NEAR[n], y=m)
        if NEAR[n] or m:
            sent[n, m] = send(near.at[n, to["y"]], here.at[NEAR[n], m], sems, (n, m), to)
    return sent, [keep(near.at[1, me["y"]], here.at[0, 0], own_sem)]


def far_first(me, send, blocks, far, sems):
    sent = []
    for n, m in FAR_TURNS:
        to = neighbour(me, z=FAR[n], y=m)
        sent.append(send(blocks.at[to["z"], to["y"]], far.at[n, m], sems, (n, m), to))
    return sent


def far_second(me, send, far, here, sems, own_sems):
    core, x = me["core"], me["x"]
    mine = core * 4 + x
    sent = {}
    for c, m in ROW:
        to = neighbour(me, core=c, x=m)
        for n in range(2):
            src = far.at[n, :, to["core"], to["x"]]
            sent[n, c, m] = send(src, here.at[FAR[n], :, mine], sems, (n, c * 4 + m), to)
    kept = [keep(far.at[n, :, core, x], here.at[FAR[n], :, mine], own_sems.at[n]) for n in range(2)]
    return sent, kept


LANES = ((0, 16), (16, 16), (32, 32))
CHUNKS = SLOTS // PER
GROUP = 8


def prepare_kernel(
    assign_ref, w_ref, g_ref, q_ref, send_ref, near, far, *refs
):
    t_refs, held, s1, r1, t = (refs[3 * n : 3 * n + 3] for n in range(5))
    gbuf, qbuf, gt, qt, wide, stage, pstage, own_part, got_part = refs[15:24]
    own_sem, hop_sem, core_sem, gsem, qsem, ssem, pair_sem, near1, far1, local_sem, out_sem, sem1 = refs[24:36]
    me = coords(lax.axis_index("node"), lax.axis_index("local"))
    copies = []
    send = sender(copies)

    def load(chunk):
        rows = pl.ds(pl.multiple_of(chunk * PER, PER), PER)
        half = lax.rem(chunk, 2)
        return (
            pltpu.make_async_copy(g_ref.at[:, rows], gbuf.at[half], gsem.at[half]),
            pltpu.make_async_copy(q_ref.at[:, rows], qbuf.at[half], qsem.at[half]),
        )

    for chunk in range(2):
        for copy in load(jnp.int32(chunk)):
            copy.start()

    own = []
    for n, (start, rows) in enumerate(LANES):
        a, b, c = (me[axis] for axis in ORDERS[n])
        own.append(
            pltpu.make_async_copy(w_ref.at[pl.ds(start, rows)], held[n].at[me["core"], a, b, c], own_sem.at[n])
        )
        own[n].start()

    met = greet(me)
    for copy in own:
        copy.wait()

    def spread(turn):
        sent = []
        for n in range(3):
            a, b, c = (me[axis] for axis in ORDERS[n])
            block = held[n].at[(me["core"], a, b, c)[: 4 - turn]]
            axis = ORDERS[n][2 - turn]
            for hop in (1, 3, 2):
                sent.append(send(block, block, hop_sem, (n, turn, hop - 1), neighbour(me, **{axis: hop})))
        return sent

    def turn_over(first, last):
        def one(chunk, carry):
            half = lax.rem(chunk, 2)
            for copy in load(chunk):
                copy.wait()
            rows = pl.ds(pl.multiple_of(chunk * PER, PER), PER)
            gt[rows] = jnp.swapaxes(gbuf[half], 0, 1)
            qt[rows] = jnp.swapaxes(qbuf[half], 0, 1)

            @pl.when(chunk + 2 < CHUNKS)
            def _():
                for copy in load(chunk + 2):
                    copy.start()

            return carry

        lax.fori_loop(first, last, one, 0)

    def pick_wide():
        def some(batch, carry):
            core, y, z_low = batch % 2, batch // 2 % 4, batch // 8
            for k in range(GROUP):
                wide[k % 2 * 2 + z_low, y, core, k // 2] = gt[assign_ref[batch * GROUP + k], :, 2 * PD : 3 * PD]
            return carry

        lax.fori_loop(0, SLOTS // GROUP, some, 0)

    def drain(buffer, sems, half):
        pltpu.make_async_copy(buffer.at[half], buffer.at[half], sems.at[half]).wait()

    def partial(slot, ref, *at):
        group = assign_ref[slot]
        g = gt[group]
        q = qt[group]
        third = lax.dot_general(q, g[:, 2 * PD : 3 * PD], MAJOR, preferred_element_type=F32)
        both = lax.dot_general(q[:, 0:W12], g[:, 0 : 2 * PD], MAJOR, preferred_element_type=F32)
        ref[(*at, slice(0, W1))] = both[0:W1, 0:PD]
        ref[(*at, slice(W1, W12))] = both[W1:W12, PD : 2 * PD]
        ref[(*at, slice(W12, WSUM))] = third[W12:WSUM]

    def to_pair(turn):
        return pltpu.make_async_remote_copy(
            src_ref=pstage.at[lax.rem(turn, 2)],
            dst_ref=got_part.at[turn],
            send_sem=pair_sem.at[0, turn],
            recv_sem=pair_sem.at[1, turn],
            device_id=place(neighbour(me, core=1)),
            device_id_type=pl.DeviceIdType.MESH,
        )

    def other_sums():
        def some(turn, carry):
            @pl.when(turn >= 2)
            def _():
                to_pair(turn - 2).wait_send()

            for k in range(GROUP):
                partial((turn * 2 + 1 - me["core"]) * GROUP + k, pstage, lax.rem(turn, 2), k)
            to_pair(turn).start()
            return carry

        lax.fori_loop(0, 8, some, 0)

    def own_sums():
        def some(turn, carry):
            for k in range(GROUP):
                partial((turn * 2 + me["core"]) * GROUP + k, own_part, turn, k)
            return carry

        lax.fori_loop(0, 8, some, 0)

    def pair_sums():
        for turn in range(8):
            to_pair(turn).wait_recv()
        sent = {}
        for n, (start, rows) in enumerate(BANDS):
            order = ORDERS[n]
            for hop in (1, 3, 2, 0):

                def add(i, carry):
                    to = {order[0]: (me[order[0]] + hop) % 4, order[1]: i // 4, order[2]: i % 4}
                    turn, k = to["z"] % 2 * 4 + to["y"], to["x"] * 2 + to["z"] // 2
                    total = own_part[turn, k, start : start + rows] + got_part[turn, k, start : start + rows]
                    if hop:
                        s1[n][hop - 1, i] = total.astype(BF)
                    else:
                        t[n][i] = total
                    return carry

                lax.fori_loop(0, 16, add, 0, unroll=4)
                if hop:
                    to = neighbour(me, **{order[0]: hop})
                    sent[n, hop] = send(s1[n].at[hop - 1], r1[n].at[hop - 1], sem1, (n, hop - 1), to)
        return sent

    def first_sums(sent):
        writes = []
        for n in range(3):
            arrive([sent[n, hop] for hop in (1, 2, 3)])

            def add(i, carry):
                t[n][i] = t[n][i] + (
                    r1[n][0, i].astype(F32) + r1[n][1, i].astype(F32) + r1[n][2, i].astype(F32)
                )
                return carry

            lax.fori_loop(0, 16, add, 0)
            writes.append(keep(t[n], t_refs[n], out_sem.at[n]))
        return writes

    def exchange_rows(core, first):
        def some(turn, carry):
            now = lax.rem(turn, 2)
            batch = turn * 2 + core
            y, z_low = turn % 4, turn // 4

            @pl.when(first + turn >= 2)
            def _():
                drain(stage, ssem, now)

            for k in range(GROUP):
                to = {"y": y, "x": k // 2, "z": k % 2 * 2 + z_low}
                g = gt[assign_ref[batch * GROUP + k]]
                w = [held[n][(core,) + tuple(to[axis] for axis in ORDERS[n])] for n in range(3)]
                none = jnp.zeros((W1, PD), BF)
                w = jnp.concatenate(
                    [
                        jnp.concatenate([w[0], none], axis=1),
                        jnp.concatenate([none, w[1]], axis=1),
                        jnp.concatenate([jnp.concatenate([none, none], axis=0), w[2]], axis=1),
                    ],
                    axis=0,
                )
                stage[now, k % 2 * 4 + k // 2] = lax.dot_general(
                    w, g[:, 0 : 2 * PD], MINOR, preferred_element_type=F32
                ).astype(BF)
            for high in range(2):
                pltpu.make_async_copy(
                    stage.at[now, pl.ds(high * 4, 4)], send_ref.at[high * 2 + z_low, y, core], ssem.at[now]
                ).start()
            return carry

        lax.fori_loop(0, SLOTS // GROUP // 2, some, 0)

    turn_over(0, 3)
    met()
    sent = spread(0)
    turn_over(3, 6)
    arrive(sent)
    sent = spread(1)
    turn_over(6, CHUNKS)
    pick_wide()
    arrive(sent)
    sent = spread(2)
    near_one = near_first(me, send, wide, near, near1, local_sem)
    far_one = far_first(me, send, wide, far, far1)
    other_sums()
    arrive(sent)
    sent = [
        send(held[n].at[me["core"]], held[n].at[me["core"]], core_sem, (n,), neighbour(me, core=1)) for n in range(3)
    ]
    own_sums()
    first = pair_sums()
    exchange_rows(me["core"], 0)
    arrive(sent)
    exchange_rows(1 - me["core"], 2)
    writes = first_sums(first)
    for half in range(2):
        drain(stage, ssem, half)
    arrive(*near_one)
    arrive(far_one)
    for turn in (6, 7):
        to_pair(turn).wait_send()
    for copy in copies:
        copy.wait_send()
    for copy in writes:
        copy.wait()


def prepare(assign, w12, grad_out, pooled):
    count = grad_out.shape[0]
    moved = [((3, 16, rows, PD), BF) for _, rows in BANDS]
    sums = [((16, rows, PD), F32) for _, rows in BANDS]
    return pl.pallas_call(
        prepare_kernel,
        in_specs=[
            pl.BlockSpec(memory_space=pltpu.SMEM),
            pl.BlockSpec(memory_space=pltpu.VMEM),
            pl.BlockSpec(memory_space=pl.ANY),
            pl.BlockSpec(memory_space=pl.ANY),
        ],
        out_specs=[pl.BlockSpec(memory_space=pl.ANY)] * 6,
        out_shape=[
            jax.ShapeDtypeStruct((4, 4, 2, 4, W12, count), BF),
            jax.ShapeDtypeStruct((2, 4, 8, count, PD), BF),
            jax.ShapeDtypeStruct((2, 4, 2, 4, count, PD), BF),
        ]
        + [jax.ShapeDtypeStruct(shape, kind) for shape, kind in sums],
        scratch_shapes=[pltpu.VMEM((2, 4, 4, 4, rows, PD), BF) for _, rows in LANES]
        + [pltpu.VMEM(shape, kind) for shape, kind in moved + moved + sums]
        + [
            pltpu.VMEM((2, count, PER, 3 * PD), BF),
            pltpu.VMEM((2, count, PER, WSUM), BF),
            pltpu.VMEM((SLOTS, count, 3 * PD), BF),
            pltpu.VMEM((SLOTS, count, WSUM), BF),
            pltpu.VMEM((4, 4, 2, 4, count, PD), BF),
            pltpu.VMEM((2, GROUP, W12, count), BF),
            pltpu.VMEM((2, GROUP, WSUM, PD), F32),
            pltpu.VMEM((8, GROUP, WSUM, PD), F32),
            pltpu.VMEM((8, GROUP, WSUM, PD), F32),
            pltpu.SemaphoreType.DMA((3,)),
            pltpu.SemaphoreType.DMA((2, 3, 3, 3)),
            pltpu.SemaphoreType.DMA((2, 3)),
            pltpu.SemaphoreType.DMA((2,)),
            pltpu.SemaphoreType.DMA((2,)),
            pltpu.SemaphoreType.DMA((2,)),
            pltpu.SemaphoreType.DMA((2, 8)),
            pltpu.SemaphoreType.DMA((2, 2, 8)),
            pltpu.SemaphoreType.DMA((2, 2, 4)),
            pltpu.SemaphoreType.DMA((2,)),
            pltpu.SemaphoreType.DMA((3,)),
            pltpu.SemaphoreType.DMA((2, 3, 3)),
        ],
        compiler_params=pltpu.CompilerParams(
            collective_id=1, has_side_effects=True, vmem_limit_bytes=62 * 2**20
        ),
        cost_estimate=pl.CostEstimate(flops=4 * 10**9, bytes_accessed=50 * 10**6, transcendentals=0),
    )(assign, w12, grad_out, pooled)


PACK = 8
LOW = ROWS // PACK


def count_columns(idx_ref, len_ref, out_ref, first, columns):
    rows = lax.broadcasted_iota(jnp.int32, (LOW, 128), 0)
    order = lax.broadcasted_iota(jnp.int32, (BAG, 128), 0)

    def column(c, carry):
        at = pl.multiple_of(c * 128, 128)
        for table in range(3):
            idx = idx_ref[table, :, pl.ds(at, 128)]
            keep = order < len_ref[table : table + 1, pl.ds(at, 128)]
            low = idx & (LOW - 1)
            unit = jnp.where(keep, lax.shift_left(jnp.ones_like(idx), 4 * lax.shift_right_logical(idx, 6)), 0)
            total = jnp.zeros((LOW, 128), jnp.int32)
            for j in range(BAG):
                total = total + jnp.where(low[j : j + 1] == rows, unit[j : j + 1], 0)
            out_ref[table, :, pl.ds(at, 128)] = total
        return carry

    lax.fori_loop(first, first + columns, column, 0)


SHARES = (40, 48, 40)
def exchange_kernel(scale, *refs):
    send_ref, near_wide, far_wide = refs[0:3]
    t, (idx_ref, len_ref, w_ref) = refs[3:6], refs[6:9]
    table_ref, proj_ref = refs[9:11]
    r2, u, r3 = (refs[11 + 3 * n : 14 + 3 * n] for n in range(3))
    counts, near, far, wide, narrow, a1, a2, a3 = refs[20:28]
    sem2, sem3 = refs[28:30]
    near1, near2, far1, far2, near_wide2, far_wide2, local_sem = refs[30:37]
    me = coords(lax.axis_index("node"), lax.axis_index("local"))
    core, y, z = me["core"], me["y"], me["z"]
    remote = []
    send = sender(remote)
    greet(me)()

    def count(share):
        count_columns(idx_ref, len_ref, counts, sum(SHARES[:share]), SHARES[share])

    a1[...] = jnp.zeros_like(a1)
    a2[...] = jnp.zeros_like(a2)
    a3[...] = jnp.zeros_like(a3)

    def hits(table, slots):
        words = jnp.concatenate(
            [counts[table, :, pl.ds(pl.multiple_of(slot * 128, 128), 128)] for slot in slots], axis=1
        )
        return jnp.concatenate(
            [(lax.shift_right_logical(words, 4 * part) & 15).astype(F32).astype(BF) for part in range(PACK)], axis=0
        )

    def match(is_wide, blocks, slots):
        if is_wide:
            a3[...] += jnp.dot(hits(2, slots), jnp.concatenate(blocks, axis=0), preferred_element_type=F32)
        else:
            both = jnp.concatenate(blocks, axis=1)
            a1[...] += lax.dot_general(hits(0, slots), both[0:W1], MINOR, preferred_element_type=F32)
            a2[...] += lax.dot_general(hits(1, slots), both[W1:W12], MINOR, preferred_element_type=F32)

    def match_near(is_wide, n, m):
        here = wide if is_wide else narrow
        from_y, from_z = (y + 4 - m) % 4, (z + 4 - NEAR[n]) % 4
        first = (from_z % 2 * 4 + from_y) * 16 + from_z // 2
        pairs = [(c, k) for c in range(2) for k in range(4)]
        match(is_wide, [here[NEAR[n], m, c * 4 + k] for c, k in pairs], [first + c * 8 + k * 2 for c, k in pairs])

    def match_far(is_wide, n, c):
        here = wide if is_wide else narrow
        from_core, from_z = (core + c) % 2, (z + 4 - FAR[n]) % 4

        def one(pair, carry):
            blocks, slots = [], []
            for i in range(2):
                m = pair * 2 + i
                from_y = (y + 4 - m) % 4
                first = ((from_z % 2 * 4 + from_y) * 2 + from_core) * 8 + from_z // 2
                for k in range(4):
                    blocks.append(here[FAR[n], m, from_core * 4 + k])
                    slots.append(first + k * 2)
            match(is_wide, blocks, slots)
            return carry

        lax.fori_loop(0, 2, one, 0)

    def near_turns(is_wide, sent, turns):
        for n, m in turns:
            if (n, m) in sent:
                sent[n, m].wait_recv()
            match_near(is_wide, n, m)

    def far_turns(is_wide, sent, kept, c):
        for n in range(2):
            arrive([sent[n, c, m] for m in range(4) if c or m], [] if c else [kept[n]])
            match_far(is_wide, n, c)

    second, third = {}, {}
    near_one = near_first(me, send, send_ref, near, near1, local_sem.at[pl.ds(0, 2)])
    far_one = far_first(me, send, send_ref, far, far1)
    for hop in (1, 3, 2):
        for n in range(3):
            at = (me[ORDERS[n][1]] + hop) % 4 * 4
            second[n, hop] = send(
                t[n].at[pl.ds(at, 4)], r2[n].at[hop - 1], sem2, (n, hop - 1), neighbour(me, **{ORDERS[n][1]: hop})
            )
    wide_near, wide_kept = near_second(me, send, near_wide, wide, near_wide2, local_sem.at[2])
    wide_far, wide_far_kept = far_second(me, send, far_wide, wide, far_wide2, local_sem.at[pl.ds(3, 2)])
    count(0)
    arrive(*near_one)
    narrow_near, narrow_kept = near_second(me, send, near, narrow, near2, local_sem.at[5])
    arrive(far_one)
    narrow_far, narrow_far_kept = far_second(me, send, far, narrow, far2, local_sem.at[pl.ds(6, 2)])
    count(1)

    for n in range(3):
        arrive([second[n, hop] for hop in (1, 2, 3)])
        at = me[ORDERS[n][1]] * 4

        def add(i, carry):
            u[n][i] = t[n][at + i] + (r2[n][0, i] + r2[n][1, i] + r2[n][2, i])
            return carry

        lax.fori_loop(0, 4, add, 0)
        for hop in (1, 3, 2):
            to = (me[ORDERS[n][2]] + hop) % 4
            third[n, hop] = send(
                u[n].at[to], r3[n].at[hop - 1], sem3, (n, hop - 1), neighbour(me, **{ORDERS[n][2]: hop})
            )

    count(2)
    arrive([], wide_kept)
    near_turns(True, wide_near, NEAR_TURNS[7:])
    near_turns(True, wide_near, NEAR_TURNS[:4])
    far_turns(True, wide_far, wide_far_kept, 0)
    near_turns(True, wide_near, NEAR_TURNS[4:7])
    far_turns(True, wide_far, wide_far_kept, 1)
    arrive([], narrow_kept)
    near_turns(False, narrow_near, NEAR_TURNS[7:])
    near_turns(False, narrow_near, NEAR_TURNS[:4])
    far_turns(False, narrow_far, narrow_far_kept, 0)
    for n, (start, rows) in enumerate(BANDS):
        arrive([third[n, hop] for hop in (1, 2, 3)])
        total = u[n][me[ORDERS[n][2]]] + (r3[n][0] + r3[n][1] + r3[n][2])
        proj_ref[start : start + rows] = total * scale
    near_turns(False, narrow_near, NEAR_TURNS[4:7])
    far_turns(False, narrow_far, narrow_far_kept, 1)

    total = a3[...]
    high = total.astype(BF)
    rest = total - high.astype(F32)
    middle = rest.astype(BF)
    last = (rest - middle.astype(F32)).astype(BF)
    w = w_ref[W12:WSUM]
    widest = sum(lax.dot_general(part, w, MINOR, preferred_element_type=F32) for part in (last, middle, high))
    table_ref[...] = jnp.concatenate([a1[...], a2[...], widest], axis=1)
    for copy in remote:
        copy.wait_send()


def exchange(send, near_wide, far_wide, sums, lookups, lengths, weights, scale):
    total = lookups.shape[2]

    def each(*lead):
        return [pltpu.VMEM(lead + (rows, PD), F32) for _, rows in BANDS]

    count = send.shape[-1]
    return pl.pallas_call(
        functools.partial(exchange_kernel, scale),
        in_specs=[pl.BlockSpec(memory_space=pl.ANY)] * 3 + [pl.BlockSpec(memory_space=pltpu.VMEM)] * 6,
        out_specs=[pl.BlockSpec(memory_space=pltpu.VMEM)] * 2,
        out_shape=[
            jax.ShapeDtypeStruct((ROWS, WSUM), F32),
            jax.ShapeDtypeStruct((WSUM, PD), F32),
        ],
        scratch_shapes=[
            *each(3, 4),
            *each(4),
            *each(3),
            pltpu.VMEM((3, LOW, total), jnp.int32),
            pltpu.VMEM((2, 4, 8, W12, count), BF),
            pltpu.VMEM((2, 4, 2, 4, W12, count), BF),
            pltpu.VMEM((4, 4, 8, count, PD), BF),
            pltpu.VMEM((4, 4, 8, W12, count), BF),
            pltpu.VMEM((ROWS, W1), F32),
            pltpu.VMEM((ROWS, W2), F32),
            pltpu.VMEM((ROWS, PD), F32),
            pltpu.SemaphoreType.DMA((2, 3, 3)),
            pltpu.SemaphoreType.DMA((2, 3, 3)),
            pltpu.SemaphoreType.DMA((2, 2, 8)),
            pltpu.SemaphoreType.DMA((2, 2, 4)),
            pltpu.SemaphoreType.DMA((2, 2, 4)),
            pltpu.SemaphoreType.DMA((2, 2, 8)),
            pltpu.SemaphoreType.DMA((2, 2, 4)),
            pltpu.SemaphoreType.DMA((2, 2, 8)),
            pltpu.SemaphoreType.DMA((8,)),
        ],
        compiler_params=pltpu.CompilerParams(
            collective_id=0, has_side_effects=True, vmem_limit_bytes=62 * 2**20
        ),
        cost_estimate=pl.CostEstimate(flops=10**10, bytes_accessed=60 * 10**6, transcendentals=0),
    )(send, near_wide, far_wide, *sums, lookups, lengths, weights)


def local(grad_out, pooled, proj, assign, indices, lengths):
    scale = 1.0 / math.sqrt(grad_out.shape[0] * SLOTS)
    send, near, far, *sums = prepare(assign, proj[0, :W12], grad_out, pooled)
    lookups = jnp.transpose(indices[0], (1, 2, 0))
    table_grad, proj_grad = exchange(
        send, near, far, sums, lookups, jnp.transpose(lengths[0], (1, 0)), proj[0], scale
    )
    return (table_grad[None], proj_grad[None])


def solution(mesh):
    placed = (
        P(("node", "local"), None, None),
        P(("node", "local"), None, None),
        P(("node", "local"), None, None),
        P(),
        P(("node", "local"), None, None, None),
        P(("node", "local"), None, None),
    )
    return jax.shard_map(
        local,
        mesh=mesh,
        in_specs=placed,
        out_specs=(P(("node", "local"), None, None), P(("node", "local"), None, None)),
        check_vma=False,
    )
```

```python
import functools
import math

import jax
import jax.numpy as jnp
from jax import lax
from jax.experimental import pallas as pl
from jax.experimental.pallas import tpu as pltpu
from jax.sharding import PartitionSpec as P

ROWS = 512
W1 = 16
W2 = 48
W3 = 192
W12 = W1 + W2
WSUM = W12 + W3
PD = 128
BAG = 8
SLOTS = 128
PER = 16
BANDS = ((0, 96), (96, 80), (176, 80))
ORDERS = (("z", "y", "x"), ("y", "x", "z"), ("x", "z", "y"))
BF = jnp.bfloat16
F32 = jnp.float32
MINOR = (((1,), (1,)), ((), ()))
MAJOR = (((0,), (0,)), ((), ()))


def coords(node, local):
    return {
        "core": node % 2,
        "y": node // 2 % 4,
        "x": local // 2,
        "z": local % 2 * 2 + node // 8,
    }


def place(at):
    return {
        "node": (at["z"] % 2 * 4 + at["y"]) * 2 + at["core"],
        "local": at["x"] * 2 + at["z"] // 2,
    }


NEAR = (2, 0)
FAR = (1, 3)
NEAR_TURNS = ((0, 1), (1, 3), (0, 3), (1, 1), (0, 2), (1, 2), (0, 0), (1, 0))
FAR_TURNS = ((0, 1), (1, 3), (1, 1), (0, 3), (0, 2), (1, 2), (0, 0), (1, 0))
ROW = tuple((c, m) for c in range(2) for m in (1, 3, 2, 0) if c or m)


def neighbour(me, **hops):
    at = dict(me)
    for axis, hop in hops.items():
        at[axis] = (me[axis] + hop) % (2 if axis == "core" else 4)
    return at


def greet(me):
    partners = [neighbour(me, core=c, x=m) for c, m in ROW]
    partners += [neighbour(me, z=n // 4, y=n % 4) for n in range(1, 16)]
    barrier = pltpu.get_barrier_semaphore()
    for partner in partners:
        pl.semaphore_signal(barrier, inc=1, device_id=place(partner), device_id_type=pl.DeviceIdType.MESH)
    return lambda: pl.semaphore_wait(barrier, len(partners))


def sender(remote):
    def send(src, dst, sems, at, to):
        copy = pltpu.make_async_remote_copy(
            src_ref=src,
            dst_ref=dst,
            send_sem=sems.at[(0,) + at],
            recv_sem=sems.at[(1,) + at],
            device_id=place(to),
            device_id_type=pl.DeviceIdType.MESH,
        )
        copy.start()
        remote.append(copy)
        return copy

    return send


def keep(src, dst, sem):
    copy = pltpu.make_async_copy(src, dst, sem)
    copy.start()
    return copy


def arrive(sent, kept=()):
    for copy in sent:
        copy.wait_recv()
    for copy in kept:
        copy.wait()


def near_first(me, send, blocks, near, sems, own_sems):
    core, x, z = me["core"], me["x"], me["z"]
    mine = core * 4 + x
    sent = []
    for c, m in ROW:
        to = neighbour(me, core=c, x=m)
        for n in range(2):
            src = blocks.at[(z + NEAR[n]) % 4, :, to["core"], to["x"]]
            sent.append(send(src, near.at[n, :, mine], sems, (n, c * 4 + m), to))
    kept = [
        keep(blocks.at[(z + NEAR[n]) % 4, :, core, x], near.at[n, :, mine], own_sems.at[n]) for n in range(2)
    ]
    return sent, kept


def near_second(me, send, near, here, sems, own_sem):
    sent = {}
    for n, m in NEAR_TURNS:
        to = neighbour(me, z=NEAR[n], y=m)
        if NEAR[n] or m:
            sent[n, m] = send(near.at[n, to["y"]], here.at[NEAR[n], m], sems, (n, m), to)
    return sent, [keep(near.at[1, me["y"]], here.at[0, 0], own_sem)]


def far_first(me, send, blocks, far, sems):
    sent = []
    for n, m in FAR_TURNS:
        to = neighbour(me, z=FAR[n], y=m)
        sent.append(send(blocks.at[to["z"], to["y"]], far.at[n, m], sems, (n, m), to))
    return sent


def far_second(me, send, far, here, sems, own_sems):
    core, x = me["core"], me["x"]
    mine = core * 4 + x
    sent = {}
    for c, m in ROW:
        to = neighbour(me, core=c, x=m)
        for n in range(2):
            src = far.at[n, :, to["core"], to["x"]]
            sent[n, c, m] = send(src, here.at[FAR[n], :, mine], sems, (n, c * 4 + m), to)
    kept = [keep(far.at[n, :, core, x], here.at[FAR[n], :, mine], own_sems.at[n]) for n in range(2)]
    return sent, kept


LANES = ((0, 16), (16, 16), (32, 32))
CHUNKS = SLOTS // PER
GROUP = 8


def prepare_kernel(
    assign_ref, w_ref, g_ref, q_ref, send_ref, near, far, *refs
):
    t_refs, held, s1, r1, t = (refs[3 * n : 3 * n + 3] for n in range(5))
    gbuf, qbuf, gt, qt, wide, stage, pstage, own_part, got_part = refs[15:24]
    buf3, gt3, sem3 = refs[36:39]
    own_sem, hop_sem, core_sem, gsem, qsem, ssem, pair_sem, near1, far1, local_sem, out_sem, sem1 = refs[24:36]
    me = coords(lax.axis_index("node"), lax.axis_index("local"))
    copies = []
    send = sender(copies)

    def load(chunk):
        rows = pl.ds(pl.multiple_of(chunk * PER, PER), PER)
        half = lax.rem(chunk, 2)
        return (
            pltpu.make_async_copy(g_ref.at[:, rows, pl.ds(0, 2 * PD)], gbuf.at[half], gsem.at[half]),
            pltpu.make_async_copy(q_ref.at[:, rows], qbuf.at[half], qsem.at[half]),
        )

    def load3(chunk):
        rows = pl.ds(pl.multiple_of(chunk * PER, PER), PER)
        part = lax.rem(chunk, 4)
        return pltpu.make_async_copy(g_ref.at[:, rows, pl.ds(2 * PD, PD)], buf3.at[part], sem3.at[part])

    for chunk in range(4):
        load3(jnp.int32(chunk)).start()
    for chunk in range(2):
        for copy in load(jnp.int32(chunk)):
            copy.start()

    own = []
    for n, (start, rows) in enumerate(LANES):
        a, b, c = (me[axis] for axis in ORDERS[n])
        own.append(
            pltpu.make_async_copy(w_ref.at[pl.ds(start, rows)], held[n].at[me["core"], a, b, c], own_sem.at[n])
        )
        own[n].start()

    met = greet(me)
    for copy in own:
        copy.wait()

    def spread(turn):
        sent = []
        for n in range(3):
            a, b, c = (me[axis] for axis in ORDERS[n])
            block = held[n].at[(me["core"], a, b, c)[: 4 - turn]]
            axis = ORDERS[n][2 - turn]
            for hop in (1, 3, 2):
                sent.append(send(block, block, hop_sem, (n, turn, hop - 1), neighbour(me, **{axis: hop})))
        return sent

    def turn_third():
        def one(chunk, carry):
            load3(chunk).wait()
            gt3[pl.ds(pl.multiple_of(chunk * PER, PER), PER)] = jnp.swapaxes(buf3[lax.rem(chunk, 4)], 0, 1)

            @pl.when(chunk + 4 < CHUNKS)
            def _():
                load3(chunk + 4).start()

            return carry

        lax.fori_loop(0, CHUNKS, one, 0)

    def turn_over(first, last):
        def one(chunk, carry):
            half = lax.rem(chunk, 2)
            for copy in load(chunk):
                copy.wait()
            rows = pl.ds(pl.multiple_of(chunk * PER, PER), PER)
            gt[rows] = jnp.swapaxes(gbuf[half], 0, 1)
            qt[rows] = jnp.swapaxes(qbuf[half], 0, 1)

            @pl.when(chunk + 2 < CHUNKS)
            def _():
                for copy in load(chunk + 2):
                    copy.start()

            return carry

        lax.fori_loop(first, last, one, 0)

    def pick_wide():
        def some(batch, carry):
            core, y, z_low = batch % 2, batch // 2 % 4, batch // 8
            for k in range(GROUP):
                wide[k % 2 * 2 + z_low, y, core, k // 2] = gt3[assign_ref[batch * GROUP + k]]
            return carry

        lax.fori_loop(0, SLOTS // GROUP, some, 0)

    def drain(buffer, sems, half):
        pltpu.make_async_copy(buffer.at[half], buffer.at[half], sems.at[half]).wait()

    def partial(slot, ref, *at):
        group = assign_ref[slot]
        g = gt[group]
        q = qt[group]
        third = lax.dot_general(q, gt3[group], MAJOR, preferred_element_type=F32)
        both = lax.dot_general(q[:, 0:W12], g, MAJOR, preferred_element_type=F32)
        ref[(*at, slice(0, W1))] = both[0:W1, 0:PD]
        ref[(*at, slice(W1, W12))] = both[W1:W12, PD : 2 * PD]
        ref[(*at, slice(W12, WSUM))] = third[W12:WSUM]

    def to_pair(turn):
        return pltpu.make_async_remote_copy(
            src_ref=pstage.at[lax.rem(turn, 2)],
            dst_ref=got_part.at[turn],
            send_sem=pair_sem.at[0, turn],
            recv_sem=pair_sem.at[1, turn],
            device_id=place(neighbour(me, core=1)),
            device_id_type=pl.DeviceIdType.MESH,
        )

    def other_sums():
        def some(turn, carry):
            @pl.when(turn >= 2)
            def _():
                to_pair(turn - 2).wait_send()

            for k in range(GROUP):
                partial((turn * 2 + 1 - me["core"]) * GROUP + k, pstage, lax.rem(turn, 2), k)
            to_pair(turn).start()
            return carry

        lax.fori_loop(0, 8, some, 0)

    def own_sums():
        def some(turn, carry):
            for k in range(GROUP):
                partial((turn * 2 + me["core"]) * GROUP + k, own_part, turn, k)
            return carry

        lax.fori_loop(0, 8, some, 0)

    def pair_sums():
        for turn in range(8):
            to_pair(turn).wait_recv()
        sent = {}
        for n, (start, rows) in enumerate(BANDS):
            order = ORDERS[n]
            for hop in (1, 3, 2, 0):

                def add(i, carry):
                    to = {order[0]: (me[order[0]] + hop) % 4, order[1]: i // 4, order[2]: i % 4}
                    turn, k = to["z"] % 2 * 4 + to["y"], to["x"] * 2 + to["z"] // 2
                    total = own_part[turn, k, start : start + rows] + got_part[turn, k, start : start + rows]
                    if hop:
                        s1[n][hop - 1, i] = total.astype(BF)
                    else:
                        t[n][i] = total
                    return carry

                lax.fori_loop(0, 16, add, 0, unroll=4)
                if hop:
                    to = neighbour(me, **{order[0]: hop})
                    sent[n, hop] = send(s1[n].at[hop - 1], r1[n].at[hop - 1], sem1, (n, hop - 1), to)
        return sent

    def first_sums(sent):
        writes = []
        for n in range(3):
            arrive([sent[n, hop] for hop in (1, 2, 3)])

            def add(i, carry):
                t[n][i] = t[n][i] + (
                    r1[n][0, i].astype(F32) + r1[n][1, i].astype(F32) + r1[n][2, i].astype(F32)
                )
                return carry

            lax.fori_loop(0, 16, add, 0)
            writes.append(keep(t[n], t_refs[n], out_sem.at[n]))
        return writes

    def exchange_rows(core, first):
        def some(turn, carry):
            now = lax.rem(turn, 2)
            batch = turn * 2 + core
            y, z_low = turn % 4, turn // 4

            @pl.when(first + turn >= 2)
            def _():
                drain(stage, ssem, now)

            for k in range(GROUP):
                to = {"y": y, "x": k // 2, "z": k % 2 * 2 + z_low}
                g = gt[assign_ref[batch * GROUP + k]]
                w = [held[n][(core,) + tuple(to[axis] for axis in ORDERS[n])] for n in range(3)]
                none = jnp.zeros((W1, PD), BF)
                w = jnp.concatenate(
                    [
                        jnp.concatenate([w[0], none], axis=1),
                        jnp.concatenate([none, w[1]], axis=1),
                        jnp.concatenate([jnp.concatenate([none, none], axis=0), w[2]], axis=1),
                    ],
                    axis=0,
                )
                stage[now, k % 2 * 4 + k // 2] = lax.dot_general(
                    w, g, MINOR, preferred_element_type=F32
                ).astype(BF)
            for high in range(2):
                pltpu.make_async_copy(
                    stage.at[now, pl.ds(high * 4, 4)], send_ref.at[high * 2 + z_low, y, core], ssem.at[now]
                ).start()
            return carry

        lax.fori_loop(0, SLOTS // GROUP // 2, some, 0)

    turn_third()
    met()
    sent = spread(0)
    pick_wide()
    near_one = near_first(me, send, wide, near, near1, local_sem)
    far_one = far_first(me, send, wide, far, far1)
    turn_over(0, CHUNKS)
    arrive(sent)
    sent = spread(1)
    other_sums()
    own_sums()
    arrive(sent)
    sent = spread(2)
    first = pair_sums()
    arrive(sent)
    sent = [
        send(held[n].at[me["core"]], held[n].at[me["core"]], core_sem, (n,), neighbour(me, core=1)) for n in range(3)
    ]
    exchange_rows(me["core"], 0)
    arrive(sent)
    exchange_rows(1 - me["core"], 2)
    writes = first_sums(first)
    for half in range(2):
        drain(stage, ssem, half)
    arrive(*near_one)
    arrive(far_one)
    for turn in (6, 7):
        to_pair(turn).wait_send()
    for copy in copies:
        copy.wait_send()
    for copy in writes:
        copy.wait()


def prepare(assign, weights, grad_out, pooled):
    count = grad_out.shape[0]
    moved = [((3, 16, rows, PD), BF) for _, rows in BANDS]
    sums = [((16, rows, PD), F32) for _, rows in BANDS]
    return pl.pallas_call(
        prepare_kernel,
        in_specs=[
            pl.BlockSpec(memory_space=pltpu.SMEM),
            pl.BlockSpec(memory_space=pl.ANY),
            pl.BlockSpec(memory_space=pl.ANY),
            pl.BlockSpec(memory_space=pl.ANY),
        ],
        out_specs=[pl.BlockSpec(memory_space=pl.ANY)] * 6,
        out_shape=[
            jax.ShapeDtypeStruct((4, 4, 2, 4, W12, count), BF),
            jax.ShapeDtypeStruct((2, 4, 8, count, PD), BF),
            jax.ShapeDtypeStruct((2, 4, 2, 4, count, PD), BF),
        ]
        + [jax.ShapeDtypeStruct(shape, kind) for shape, kind in sums],
        scratch_shapes=[pltpu.VMEM((2, 4, 4, 4, rows, PD), BF) for _, rows in LANES]
        + [pltpu.VMEM(shape, kind) for shape, kind in moved + moved + sums]
        + [
            pltpu.VMEM((2, count, PER, 2 * PD), BF),
            pltpu.VMEM((2, count, PER, WSUM), BF),
            pltpu.VMEM((SLOTS, count, 2 * PD), BF),
            pltpu.VMEM((SLOTS, count, WSUM), BF),
            pltpu.VMEM((4, 4, 2, 4, count, PD), BF),
            pltpu.VMEM((2, GROUP, W12, count), BF),
            pltpu.VMEM((2, GROUP, WSUM, PD), F32),
            pltpu.VMEM((8, GROUP, WSUM, PD), F32),
            pltpu.VMEM((8, GROUP, WSUM, PD), F32),
            pltpu.SemaphoreType.DMA((3,)),
            pltpu.SemaphoreType.DMA((2, 3, 3, 3)),
            pltpu.SemaphoreType.DMA((2, 3)),
            pltpu.SemaphoreType.DMA((2,)),
            pltpu.SemaphoreType.DMA((2,)),
            pltpu.SemaphoreType.DMA((2,)),
            pltpu.SemaphoreType.DMA((2, 8)),
            pltpu.SemaphoreType.DMA((2, 2, 8)),
            pltpu.SemaphoreType.DMA((2, 2, 4)),
            pltpu.SemaphoreType.DMA((2,)),
            pltpu.SemaphoreType.DMA((3,)),
            pltpu.SemaphoreType.DMA((2, 3, 3)),
            pltpu.VMEM((4, count, PER, PD), BF),
            pltpu.VMEM((SLOTS, count, PD), BF),
            pltpu.SemaphoreType.DMA((4,)),
        ],
        compiler_params=pltpu.CompilerParams(
            collective_id=1, has_side_effects=True, vmem_limit_bytes=62 * 2**20
        ),
        cost_estimate=pl.CostEstimate(flops=4 * 10**9, bytes_accessed=50 * 10**6, transcendentals=0),
    )(assign, weights, grad_out, pooled)


PACK = 8
LOW = ROWS // PACK


def count_columns(idx_ref, len_ref, out_ref, first, columns):
    rows = lax.broadcasted_iota(jnp.int32, (LOW, 128), 0)
    order = lax.broadcasted_iota(jnp.int32, (BAG, 128), 0)

    def column(c, carry):
        at = pl.multiple_of(c * 128, 128)
        for table in range(3):
            idx = idx_ref[table, :, pl.ds(at, 128)]
            keep = order < len_ref[table, :, pl.ds(at, 128)]
            low = idx & (LOW - 1)
            unit = jnp.where(keep, lax.shift_left(jnp.ones_like(idx), 4 * lax.shift_right_logical(idx, 6)), 0)
            total = jnp.zeros((LOW, 128), jnp.int32)
            for j in range(BAG):
                total = total + jnp.where(low[j : j + 1] == rows, unit[j : j + 1], 0)
            out_ref[table, :, pl.ds(at, 128)] = total
        return carry

    lax.fori_loop(first, first + columns, column, 0)


SHARES = (40, 48, 40)
def exchange_kernel(scale, *refs):
    send_ref, near_wide, far_wide = refs[0:3]
    t, (idx_ref, len_ref, w_ref) = refs[3:6], refs[6:9]
    table_ref, proj_ref = refs[9:11]
    r2, u, r3 = (refs[11 + 3 * n : 14 + 3 * n] for n in range(3))
    counts, near, far, wide, narrow, a1, a2, a3 = refs[20:28]
    sem2, sem3 = refs[28:30]
    near1, near2, far1, far2, near_wide2, far_wide2, local_sem = refs[30:37]
    me = coords(lax.axis_index("node"), lax.axis_index("local"))
    core, y, z = me["core"], me["y"], me["z"]
    remote = []
    send = sender(remote)
    greet(me)()

    def count(share):
        count_columns(idx_ref, len_ref, counts, sum(SHARES[:share]), SHARES[share])

    a1[...] = jnp.zeros_like(a1)
    a2[...] = jnp.zeros_like(a2)
    a3[...] = jnp.zeros_like(a3)

    def hits(table, slots):
        words = jnp.concatenate(
            [counts[table, :, pl.ds(pl.multiple_of(slot * 128, 128), 128)] for slot in slots], axis=1
        )
        return jnp.concatenate(
            [(lax.shift_right_logical(words, 4 * part) & 15).astype(F32).astype(BF) for part in range(PACK)], axis=0
        )

    def match(is_wide, blocks, slots):
        if is_wide:
            a3[...] += jnp.dot(hits(2, slots), jnp.concatenate(blocks, axis=0), preferred_element_type=F32)
        else:
            both = jnp.concatenate(blocks, axis=1)
            a1[...] += lax.dot_general(hits(0, slots), both[0:W1], MINOR, preferred_element_type=F32)
            a2[...] += lax.dot_general(hits(1, slots), both[W1:W12], MINOR, preferred_element_type=F32)

    def match_near(is_wide, n, m):
        here = wide if is_wide else narrow
        from_y, from_z = (y + 4 - m) % 4, (z + 4 - NEAR[n]) % 4
        first = (from_z % 2 * 4 + from_y) * 16 + from_z // 2
        pairs = [(c, k) for c in range(2) for k in range(4)]
        match(is_wide, [here[NEAR[n], m, c * 4 + k] for c, k in pairs], [first + c * 8 + k * 2 for c, k in pairs])

    def match_far(is_wide, n, c):
        here = wide if is_wide else narrow
        from_core, from_z = (core + c) % 2, (z + 4 - FAR[n]) % 4

        def one(pair, carry):
            blocks, slots = [], []
            for i in range(2):
                m = pair * 2 + i
                from_y = (y + 4 - m) % 4
                first = ((from_z % 2 * 4 + from_y) * 2 + from_core) * 8 + from_z // 2
                for k in range(4):
                    blocks.append(here[FAR[n], m, from_core * 4 + k])
                    slots.append(first + k * 2)
            match(is_wide, blocks, slots)
            return carry

        lax.fori_loop(0, 2, one, 0)

    def near_turns(is_wide, sent, turns):
        for n, m in turns:
            if (n, m) in sent:
                sent[n, m].wait_recv()
            match_near(is_wide, n, m)

    def far_turns(is_wide, sent, kept, c):
        for n in range(2):
            arrive([sent[n, c, m] for m in range(4) if c or m], [] if c else [kept[n]])
            match_far(is_wide, n, c)

    second, third = {}, {}
    near_one = near_first(me, send, send_ref, near, near1, local_sem.at[pl.ds(0, 2)])
    far_one = far_first(me, send, send_ref, far, far1)
    for hop in (1, 3, 2):
        for n in range(3):
            at = (me[ORDERS[n][1]] + hop) % 4 * 4
            second[n, hop] = send(
                t[n].at[pl.ds(at, 4)], r2[n].at[hop - 1], sem2, (n, hop - 1), neighbour(me, **{ORDERS[n][1]: hop})
            )
    wide_near, wide_kept = near_second(me, send, near_wide, wide, near_wide2, local_sem.at[2])
    wide_far, wide_far_kept = far_second(me, send, far_wide, wide, far_wide2, local_sem.at[pl.ds(3, 2)])
    count(0)
    arrive(*near_one)
    narrow_near, narrow_kept = near_second(me, send, near, narrow, near2, local_sem.at[5])
    arrive(far_one)
    narrow_far, narrow_far_kept = far_second(me, send, far, narrow, far2, local_sem.at[pl.ds(6, 2)])
    count(1)

    for n in range(3):
        arrive([second[n, hop] for hop in (1, 2, 3)])
        at = me[ORDERS[n][1]] * 4

        def add(i, carry):
            u[n][i] = t[n][at + i] + (r2[n][0, i] + r2[n][1, i] + r2[n][2, i])
            return carry

        lax.fori_loop(0, 4, add, 0)
        for hop in (1, 3, 2):
            to = (me[ORDERS[n][2]] + hop) % 4
            third[n, hop] = send(
                u[n].at[to], r3[n].at[hop - 1], sem3, (n, hop - 1), neighbour(me, **{ORDERS[n][2]: hop})
            )

    count(2)
    arrive([], wide_kept)
    near_turns(True, wide_near, NEAR_TURNS[7:])
    near_turns(True, wide_near, NEAR_TURNS[:4])
    far_turns(True, wide_far, wide_far_kept, 0)
    near_turns(True, wide_near, NEAR_TURNS[4:7])
    far_turns(True, wide_far, wide_far_kept, 1)
    arrive([], narrow_kept)
    near_turns(False, narrow_near, NEAR_TURNS[7:])
    near_turns(False, narrow_near, NEAR_TURNS[:4])
    far_turns(False, narrow_far, narrow_far_kept, 0)
    for n, (start, rows) in enumerate(BANDS):
        arrive([third[n, hop] for hop in (1, 2, 3)])
        total = u[n][me[ORDERS[n][2]]] + (r3[n][0] + r3[n][1] + r3[n][2])
        proj_ref[start : start + rows] = total * scale
    near_turns(False, narrow_near, NEAR_TURNS[4:7])
    far_turns(False, narrow_far, narrow_far_kept, 1)

    total = a3[...]
    high = total.astype(BF)
    rest = total - high.astype(F32)
    middle = rest.astype(BF)
    last = (rest - middle.astype(F32)).astype(BF)
    w = w_ref[W12:WSUM]
    widest = sum(lax.dot_general(part, w, MINOR, preferred_element_type=F32) for part in (last, middle, high))
    table_ref[...] = jnp.concatenate([a1[...], a2[...], widest], axis=1)
    for copy in remote:
        copy.wait_send()


def exchange(send, near_wide, far_wide, sums, lookups, lengths, weights, scale):
    total = lookups.shape[2]

    def each(*lead):
        return [pltpu.VMEM(lead + (rows, PD), F32) for _, rows in BANDS]

    count = send.shape[-1]
    return pl.pallas_call(
        functools.partial(exchange_kernel, scale),
        in_specs=[pl.BlockSpec(memory_space=pl.ANY)] * 3 + [pl.BlockSpec(memory_space=pltpu.VMEM)] * 6,
        out_specs=[pl.BlockSpec(memory_space=pltpu.VMEM)] * 2,
        out_shape=[
            jax.ShapeDtypeStruct((ROWS, WSUM), F32),
            jax.ShapeDtypeStruct((WSUM, PD), F32),
        ],
        scratch_shapes=[
            *each(3, 4),
            *each(4),
            *each(3),
            pltpu.VMEM((3, LOW, total), jnp.int32),
            pltpu.VMEM((2, 4, 8, W12, count), BF),
            pltpu.VMEM((2, 4, 2, 4, W12, count), BF),
            pltpu.VMEM((4, 4, 8, count, PD), BF),
            pltpu.VMEM((4, 4, 8, W12, count), BF),
            pltpu.VMEM((ROWS, W1), F32),
            pltpu.VMEM((ROWS, W2), F32),
            pltpu.VMEM((ROWS, PD), F32),
            pltpu.SemaphoreType.DMA((2, 3, 3)),
            pltpu.SemaphoreType.DMA((2, 3, 3)),
            pltpu.SemaphoreType.DMA((2, 2, 8)),
            pltpu.SemaphoreType.DMA((2, 2, 4)),
            pltpu.SemaphoreType.DMA((2, 2, 4)),
            pltpu.SemaphoreType.DMA((2, 2, 8)),
            pltpu.SemaphoreType.DMA((2, 2, 4)),
            pltpu.SemaphoreType.DMA((2, 2, 8)),
            pltpu.SemaphoreType.DMA((8,)),
        ],
        compiler_params=pltpu.CompilerParams(
            collective_id=0, has_side_effects=True, vmem_limit_bytes=62 * 2**20
        ),
        cost_estimate=pl.CostEstimate(flops=10**10, bytes_accessed=60 * 10**6, transcendentals=0),
    )(send, near_wide, far_wide, *sums, lookups, lengths, weights)


def local(grad_out, pooled, proj, assign, indices, lengths):
    scale = 1.0 / math.sqrt(grad_out.shape[0] * SLOTS)
    send, near, far, *sums = prepare(assign, proj[0], grad_out, pooled)
    lookups = jnp.transpose(indices[0], (1, 2, 0))
    table_grad, proj_grad = exchange(
        send, near, far, sums, lookups, jnp.transpose(lengths, (2, 0, 1)), proj[0], scale
    )
    return (table_grad[None], proj_grad[None])


def solution(mesh):
    placed = (
        P(("node", "local"), None, None),
        P(("node", "local"), None, None),
        P(("node", "local"), None, None),
        P(),
        P(("node", "local"), None, None, None),
        P(("node", "local"), None, None),
    )
    return jax.shard_map(
        local,
        mesh=mesh,
        in_specs=placed,
        out_specs=(P(("node", "local"), None, None), P(("node", "local"), None, None)),
        check_vma=False,
    )
```

```python
import functools
import math

import jax
import jax.numpy as jnp
from jax import lax
from jax.experimental import pallas as pl
from jax.experimental.pallas import tpu as pltpu
from jax.sharding import PartitionSpec as P

ROWS = 512
W1 = 16
W2 = 48
W3 = 192
W12 = W1 + W2
WSUM = W12 + W3
PD = 128
BAG = 8
SLOTS = 128
PER = 16
BANDS = ((0, 96), (96, 80), (176, 80))
ORDERS = (("z", "y", "x"), ("y", "x", "z"), ("x", "z", "y"))
BF = jnp.bfloat16
F32 = jnp.float32
MINOR = (((1,), (1,)), ((), ()))
MAJOR = (((0,), (0,)), ((), ()))


def coords(node, local):
    return {
        "core": node % 2,
        "y": node // 2 % 4,
        "x": local // 2,
        "z": local % 2 * 2 + node // 8,
    }


def place(at):
    return {
        "node": (at["z"] % 2 * 4 + at["y"]) * 2 + at["core"],
        "local": at["x"] * 2 + at["z"] // 2,
    }


NEAR = (2, 0)
FAR = (1, 3)
NEAR_TURNS = ((0, 1), (1, 3), (0, 3), (1, 1), (0, 2), (1, 2), (0, 0), (1, 0))
FAR_TURNS = ((0, 1), (1, 3), (1, 1), (0, 3), (0, 2), (1, 2), (0, 0), (1, 0))
ROW = tuple((c, m) for c in range(2) for m in (1, 3, 2, 0) if c or m)


def neighbour(me, **hops):
    at = dict(me)
    for axis, hop in hops.items():
        at[axis] = (me[axis] + hop) % (2 if axis == "core" else 4)
    return at


def greet(me):
    partners = [neighbour(me, core=c, x=m) for c, m in ROW]
    partners += [neighbour(me, z=n // 4, y=n % 4) for n in range(1, 16)]
    barrier = pltpu.get_barrier_semaphore()
    for partner in partners:
        pl.semaphore_signal(barrier, inc=1, device_id=place(partner), device_id_type=pl.DeviceIdType.MESH)
    return lambda: pl.semaphore_wait(barrier, len(partners))


def sender(remote):
    def send(src, dst, sems, at, to):
        copy = pltpu.make_async_remote_copy(
            src_ref=src,
            dst_ref=dst,
            send_sem=sems.at[(0,) + at],
            recv_sem=sems.at[(1,) + at],
            device_id=place(to),
            device_id_type=pl.DeviceIdType.MESH,
        )
        copy.start()
        remote.append(copy)
        return copy

    return send


def keep(src, dst, sem):
    copy = pltpu.make_async_copy(src, dst, sem)
    copy.start()
    return copy


def arrive(sent, kept=()):
    for copy in sent:
        copy.wait_recv()
    for copy in kept:
        copy.wait()


def near_first(me, send, blocks, near, sems, own_sems):
    core, x, z = me["core"], me["x"], me["z"]
    mine = core * 4 + x
    sent = []
    for c, m in ROW:
        to = neighbour(me, core=c, x=m)
        for n in range(2):
            src = blocks.at[(z + NEAR[n]) % 4, :, to["core"], to["x"]]
            sent.append(send(src, near.at[n, :, mine], sems, (n, c * 4 + m), to))
    kept = [
        keep(blocks.at[(z + NEAR[n]) % 4, :, core, x], near.at[n, :, mine], own_sems.at[n]) for n in range(2)
    ]
    return sent, kept


def near_second(me, send, near, here, sems, own_sem):
    sent = {}
    for n, m in NEAR_TURNS:
        to = neighbour(me, z=NEAR[n], y=m)
        if NEAR[n] or m:
            sent[n, m] = send(near.at[n, to["y"]], here.at[NEAR[n], m], sems, (n, m), to)
    return sent, [keep(near.at[1, me["y"]], here.at[0, 0], own_sem)]


def far_first(me, send, blocks, far, sems):
    sent = []
    for n, m in FAR_TURNS:
        to = neighbour(me, z=FAR[n], y=m)
        sent.append(send(blocks.at[to["z"], to["y"]], far.at[n, m], sems, (n, m), to))
    return sent


def far_second(me, send, far, here, sems, own_sems):
    core, x = me["core"], me["x"]
    mine = core * 4 + x
    sent = {}
    for c, m in ROW:
        to = neighbour(me, core=c, x=m)
        for n in range(2):
            src = far.at[n, :, to["core"], to["x"]]
            sent[n, c, m] = send(src, here.at[FAR[n], :, mine], sems, (n, c * 4 + m), to)
    kept = [keep(far.at[n, :, core, x], here.at[FAR[n], :, mine], own_sems.at[n]) for n in range(2)]
    return sent, kept


LANES = ((0, 16), (16, 16), (32, 32))
CHUNKS = SLOTS // PER
GROUP = 8


def prepare_kernel(
    assign_ref, w_ref, g_ref, q_ref, send_ref, near, far, *refs
):
    t_refs, held, s1, r1, t = (refs[3 * n : 3 * n + 3] for n in range(5))
    gbuf, qbuf, gt, qt, wide, stage, pstage, own_part, got_part = refs[15:24]
    buf3, gt3, sem3 = refs[36:39]
    own_sem, hop_sem, core_sem, gsem, qsem, ssem, pair_sem, near1, far1, local_sem, out_sem, sem1 = refs[24:36]
    me = coords(lax.axis_index("node"), lax.axis_index("local"))
    copies = []
    send = sender(copies)

    def load(chunk):
        rows = pl.ds(pl.multiple_of(chunk * PER, PER), PER)
        half = lax.rem(chunk, 2)
        return (
            pltpu.make_async_copy(g_ref.at[:, rows, pl.ds(0, 2 * PD)], gbuf.at[half], gsem.at[half]),
            pltpu.make_async_copy(q_ref.at[:, rows], qbuf.at[half], qsem.at[half]),
        )

    def load3(chunk):
        rows = pl.ds(pl.multiple_of(chunk * PER, PER), PER)
        part = lax.rem(chunk, 4)
        return pltpu.make_async_copy(g_ref.at[:, rows, pl.ds(2 * PD, PD)], buf3.at[part], sem3.at[part])

    for chunk in range(4):
        load3(jnp.int32(chunk)).start()
    for chunk in range(2):
        for copy in load(jnp.int32(chunk)):
            copy.start()

    own = []
    for n, (start, rows) in enumerate(LANES):
        a, b, c = (me[axis] for axis in ORDERS[n])
        own.append(
            pltpu.make_async_copy(w_ref.at[pl.ds(start, rows)], held[n].at[me["core"], a, b, c], own_sem.at[n])
        )
        own[n].start()

    met = greet(me)
    for copy in own:
        copy.wait()

    def spread(turn):
        sent = []
        for n in range(3):
            a, b, c = (me[axis] for axis in ORDERS[n])
            block = held[n].at[(me["core"], a, b, c)[: 4 - turn]]
            axis = ORDERS[n][2 - turn]
            for hop in (1, 3, 2):
                sent.append(send(block, block, hop_sem, (n, turn, hop - 1), neighbour(me, **{axis: hop})))
        return sent

    def turn_third():
        def one(chunk, carry):
            load3(chunk).wait()
            gt3[pl.ds(pl.multiple_of(chunk * PER, PER), PER)] = jnp.swapaxes(buf3[lax.rem(chunk, 4)], 0, 1)

            @pl.when(chunk + 4 < CHUNKS)
            def _():
                load3(chunk + 4).start()

            return carry

        lax.fori_loop(0, CHUNKS, one, 0)

    def turn_over(first, last):
        def one(chunk, carry):
            half = lax.rem(chunk, 2)
            for copy in load(chunk):
                copy.wait()
            rows = pl.ds(pl.multiple_of(chunk * PER, PER), PER)
            gt[rows] = jnp.swapaxes(gbuf[half], 0, 1)
            qt[rows] = jnp.swapaxes(qbuf[half], 0, 1)

            @pl.when(chunk + 2 < CHUNKS)
            def _():
                for copy in load(chunk + 2):
                    copy.start()

            return carry

        lax.fori_loop(first, last, one, 0)

    def pick_wide():
        def some(batch, carry):
            core, y, z_low = batch % 2, batch // 2 % 4, batch // 8
            for k in range(GROUP):
                wide[k % 2 * 2 + z_low, y, core, k // 2] = gt3[assign_ref[batch * GROUP + k]]
            return carry

        lax.fori_loop(0, SLOTS // GROUP, some, 0)

    def drain(buffer, sems, half):
        pltpu.make_async_copy(buffer.at[half], buffer.at[half], sems.at[half]).wait()

    def partial(slot, ref, *at):
        group = assign_ref[slot]
        g = gt[group]
        q = qt[group]
        third = lax.dot_general(q, gt3[group], MAJOR, preferred_element_type=F32)
        both = lax.dot_general(q[:, 0:W12], g, MAJOR, preferred_element_type=F32)
        ref[(*at, slice(0, W1))] = both[0:W1, 0:PD]
        ref[(*at, slice(W1, W12))] = both[W1:W12, PD : 2 * PD]
        ref[(*at, slice(W12, WSUM))] = third[W12:WSUM]

    def to_pair(turn):
        return pltpu.make_async_remote_copy(
            src_ref=pstage.at[lax.rem(turn, 2)],
            dst_ref=got_part.at[turn],
            send_sem=pair_sem.at[0, turn],
            recv_sem=pair_sem.at[1, turn],
            device_id=place(neighbour(me, core=1)),
            device_id_type=pl.DeviceIdType.MESH,
        )

    def other_sums():
        def some(turn, carry):
            @pl.when(turn >= 2)
            def _():
                to_pair(turn - 2).wait_send()

            for k in range(GROUP):
                partial((turn * 2 + 1 - me["core"]) * GROUP + k, pstage, lax.rem(turn, 2), k)
            to_pair(turn).start()
            return carry

        lax.fori_loop(0, 8, some, 0)

    def own_sums():
        def some(turn, carry):
            for k in range(GROUP):
                partial((turn * 2 + me["core"]) * GROUP + k, own_part, turn, k)
            return carry

        lax.fori_loop(0, 8, some, 0)

    def pair_sums():
        for turn in range(8):
            to_pair(turn).wait_recv()
        sent = {}
        for hop in (1, 3, 2, 0):
            for n, (start, rows) in enumerate(BANDS):
                order = ORDERS[n]

                def add(i, carry):
                    to = {order[0]: (me[order[0]] + hop) % 4, order[1]: i // 4, order[2]: i % 4}
                    turn, k = to["z"] % 2 * 4 + to["y"], to["x"] * 2 + to["z"] // 2
                    total = own_part[turn, k, start : start + rows] + got_part[turn, k, start : start + rows]
                    if hop:
                        s1[n][hop - 1, i] = total.astype(BF)
                    else:
                        t[n][i] = total
                    return carry

                lax.fori_loop(0, 16, add, 0, unroll=4)
                if hop:
                    to = neighbour(me, **{order[0]: hop})
                    sent[n, hop] = send(s1[n].at[hop - 1], r1[n].at[hop - 1], sem1, (n, hop - 1), to)
        return sent

    def first_sums(sent):
        writes = []
        for n in range(3):
            arrive([sent[n, hop] for hop in (1, 2, 3)])

            def add(i, carry):
                t[n][i] = t[n][i] + (
                    r1[n][0, i].astype(F32) + r1[n][1, i].astype(F32) + r1[n][2, i].astype(F32)
                )
                return carry

            lax.fori_loop(0, 16, add, 0)
            writes.append(keep(t[n], t_refs[n], out_sem.at[n]))
        return writes

    def exchange_rows(core, first):
        def some(turn, carry):
            now = lax.rem(turn, 2)
            batch = turn * 2 + core
            y, z_low = turn % 4, turn // 4

            @pl.when(first + turn >= 2)
            def _():
                drain(stage, ssem, now)

            for k in range(GROUP):
                to = {"y": y, "x": k // 2, "z": k % 2 * 2 + z_low}
                g = gt[assign_ref[batch * GROUP + k]]
                w = [held[n][(core,) + tuple(to[axis] for axis in ORDERS[n])] for n in range(3)]
                none = jnp.zeros((W1, PD), BF)
                w = jnp.concatenate(
                    [
                        jnp.concatenate([w[0], none], axis=1),
                        jnp.concatenate([none, w[1]], axis=1),
                        jnp.concatenate([jnp.concatenate([none, none], axis=0), w[2]], axis=1),
                    ],
                    axis=0,
                )
                stage[now, k % 2 * 4 + k // 2] = lax.dot_general(
                    w, g, MINOR, preferred_element_type=F32
                ).astype(BF)
            for high in range(2):
                pltpu.make_async_copy(
                    stage.at[now, pl.ds(high * 4, 4)], send_ref.at[high * 2 + z_low, y, core], ssem.at[now]
                ).start()
            return carry

        lax.fori_loop(0, SLOTS // GROUP // 2, some, 0)

    turn_third()
    met()
    sent = spread(0)
    pick_wide()
    near_one = near_first(me, send, wide, near, near1, local_sem)
    far_one = far_first(me, send, wide, far, far1)
    turn_over(0, CHUNKS)
    arrive(sent)
    sent = spread(1)
    other_sums()
    own_sums()
    arrive(sent)
    sent = spread(2)
    first = pair_sums()
    arrive(sent)
    sent = [
        send(held[n].at[me["core"]], held[n].at[me["core"]], core_sem, (n,), neighbour(me, core=1)) for n in range(3)
    ]
    exchange_rows(me["core"], 0)
    arrive(sent)
    exchange_rows(1 - me["core"], 2)
    writes = first_sums(first)
    for half in range(2):
        drain(stage, ssem, half)
    arrive(*near_one)
    arrive(far_one)
    for turn in (6, 7):
        to_pair(turn).wait_send()
    for copy in copies:
        copy.wait_send()
    for copy in writes:
        copy.wait()


def prepare(assign, weights, grad_out, pooled):
    count = grad_out.shape[0]
    moved = [((3, 16, rows, PD), BF) for _, rows in BANDS]
    sums = [((16, rows, PD), F32) for _, rows in BANDS]
    return pl.pallas_call(
        prepare_kernel,
        in_specs=[
            pl.BlockSpec(memory_space=pltpu.SMEM),
            pl.BlockSpec(memory_space=pl.ANY),
            pl.BlockSpec(memory_space=pl.ANY),
            pl.BlockSpec(memory_space=pl.ANY),
        ],
        out_specs=[pl.BlockSpec(memory_space=pl.ANY)] * 6,
        out_shape=[
            jax.ShapeDtypeStruct((4, 4, 2, 4, W12, count), BF),
            jax.ShapeDtypeStruct((2, 4, 8, count, PD), BF),
            jax.ShapeDtypeStruct((2, 4, 2, 4, count, PD), BF),
        ]
        + [jax.ShapeDtypeStruct(shape, kind) for shape, kind in sums],
        scratch_shapes=[pltpu.VMEM((2, 4, 4, 4, rows, PD), BF) for _, rows in LANES]
        + [pltpu.VMEM(shape, kind) for shape, kind in moved + moved + sums]
        + [
            pltpu.VMEM((2, count, PER, 2 * PD), BF),
            pltpu.VMEM((2, count, PER, WSUM), BF),
            pltpu.VMEM((SLOTS, count, 2 * PD), BF),
            pltpu.VMEM((SLOTS, count, WSUM), BF),
            pltpu.VMEM((4, 4, 2, 4, count, PD), BF),
            pltpu.VMEM((2, GROUP, W12, count), BF),
            pltpu.VMEM((2, GROUP, WSUM, PD), F32),
            pltpu.VMEM((8, GROUP, WSUM, PD), F32),
            pltpu.VMEM((8, GROUP, WSUM, PD), F32),
            pltpu.SemaphoreType.DMA((3,)),
            pltpu.SemaphoreType.DMA((2, 3, 3, 3)),
            pltpu.SemaphoreType.DMA((2, 3)),
            pltpu.SemaphoreType.DMA((2,)),
            pltpu.SemaphoreType.DMA((2,)),
            pltpu.SemaphoreType.DMA((2,)),
            pltpu.SemaphoreType.DMA((2, 8)),
            pltpu.SemaphoreType.DMA((2, 2, 8)),
            pltpu.SemaphoreType.DMA((2, 2, 4)),
            pltpu.SemaphoreType.DMA((2,)),
            pltpu.SemaphoreType.DMA((3,)),
            pltpu.SemaphoreType.DMA((2, 3, 3)),
            pltpu.VMEM((4, count, PER, PD), BF),
            pltpu.VMEM((SLOTS, count, PD), BF),
            pltpu.SemaphoreType.DMA((4,)),
        ],
        compiler_params=pltpu.CompilerParams(
            collective_id=1, has_side_effects=True, vmem_limit_bytes=62 * 2**20
        ),
        cost_estimate=pl.CostEstimate(flops=4 * 10**9, bytes_accessed=50 * 10**6, transcendentals=0),
    )(assign, weights, grad_out, pooled)


PACK = 8
LOW = ROWS // PACK


def count_columns(idx_ref, len_ref, out_ref, first, columns):
    rows = lax.broadcasted_iota(jnp.int32, (LOW, 128), 0)
    order = lax.broadcasted_iota(jnp.int32, (BAG, 128), 0)

    def column(c, carry):
        at = pl.multiple_of(c * 128, 128)
        for table in range(3):
            idx = idx_ref[table, :, pl.ds(at, 128)]
            keep = order < len_ref[table, :, pl.ds(at, 128)]
            low = idx & (LOW - 1)
            unit = jnp.where(keep, lax.shift_left(jnp.ones_like(idx), 4 * lax.shift_right_logical(idx, 6)), 0)
            total = jnp.zeros((LOW, 128), jnp.int32)
            for j in range(BAG):
                total = total + jnp.where(low[j : j + 1] == rows, unit[j : j + 1], 0)
            out_ref[table, :, pl.ds(at, 128)] = total
        return carry

    lax.fori_loop(first, first + columns, column, 0)


SHARES = (40, 48, 40)
def exchange_kernel(scale, *refs):
    send_ref, near_wide, far_wide = refs[0:3]
    t, (idx_ref, len_ref, w_ref) = refs[3:6], refs[6:9]
    table_ref, proj_ref = refs[9:11]
    r2, u, r3 = (refs[11 + 3 * n : 14 + 3 * n] for n in range(3))
    counts, near, far, wide, narrow, a1, a2, a3 = refs[20:28]
    sem2, sem3 = refs[28:30]
    near1, near2, far1, far2, near_wide2, far_wide2, local_sem = refs[30:37]
    me = coords(lax.axis_index("node"), lax.axis_index("local"))
    core, y, z = me["core"], me["y"], me["z"]
    remote = []
    send = sender(remote)
    greet(me)()

    def count(share):
        count_columns(idx_ref, len_ref, counts, sum(SHARES[:share]), SHARES[share])

    a1[...] = jnp.zeros_like(a1)
    a2[...] = jnp.zeros_like(a2)
    a3[...] = jnp.zeros_like(a3)

    def hits(table, slots):
        words = jnp.concatenate(
            [counts[table, :, pl.ds(pl.multiple_of(slot * 128, 128), 128)] for slot in slots], axis=1
        )
        return jnp.concatenate(
            [(lax.shift_right_logical(words, 4 * part) & 15).astype(F32).astype(BF) for part in range(PACK)], axis=0
        )

    def match(is_wide, blocks, slots):
        if is_wide:
            a3[...] += jnp.dot(hits(2, slots), jnp.concatenate(blocks, axis=0), preferred_element_type=F32)
        else:
            both = jnp.concatenate(blocks, axis=1)
            a1[...] += lax.dot_general(hits(0, slots), both[0:W1], MINOR, preferred_element_type=F32)
            a2[...] += lax.dot_general(hits(1, slots), both[W1:W12], MINOR, preferred_element_type=F32)

    def match_near(is_wide, n, m):
        here = wide if is_wide else narrow
        from_y, from_z = (y + 4 - m) % 4, (z + 4 - NEAR[n]) % 4
        first = (from_z % 2 * 4 + from_y) * 16 + from_z // 2
        pairs = [(c, k) for c in range(2) for k in range(4)]
        match(is_wide, [here[NEAR[n], m, c * 4 + k] for c, k in pairs], [first + c * 8 + k * 2 for c, k in pairs])

    def match_far(is_wide, n, c):
        here = wide if is_wide else narrow
        from_core, from_z = (core + c) % 2, (z + 4 - FAR[n]) % 4

        def one(pair, carry):
            blocks, slots = [], []
            for i in range(2):
                m = pair * 2 + i
                from_y = (y + 4 - m) % 4
                first = ((from_z % 2 * 4 + from_y) * 2 + from_core) * 8 + from_z // 2
                for k in range(4):
                    blocks.append(here[FAR[n], m, from_core * 4 + k])
                    slots.append(first + k * 2)
            match(is_wide, blocks, slots)
            return carry

        lax.fori_loop(0, 2, one, 0)

    def near_turns(is_wide, sent, turns):
        for n, m in turns:
            if (n, m) in sent:
                sent[n, m].wait_recv()
            match_near(is_wide, n, m)

    def far_turns(is_wide, sent, kept, c):
        for n in range(2):
            arrive([sent[n, c, m] for m in range(4) if c or m], [] if c else [kept[n]])
            match_far(is_wide, n, c)

    second, third = {}, {}
    near_one = near_first(me, send, send_ref, near, near1, local_sem.at[pl.ds(0, 2)])
    far_one = far_first(me, send, send_ref, far, far1)
    for hop in (1, 3, 2):
        for n in range(3):
            at = (me[ORDERS[n][1]] + hop) % 4 * 4
            second[n, hop] = send(
                t[n].at[pl.ds(at, 4)], r2[n].at[hop - 1], sem2, (n, hop - 1), neighbour(me, **{ORDERS[n][1]: hop})
            )
    wide_near, wide_kept = near_second(me, send, near_wide, wide, near_wide2, local_sem.at[2])
    wide_far, wide_far_kept = far_second(me, send, far_wide, wide, far_wide2, local_sem.at[pl.ds(3, 2)])
    count(0)
    arrive(*near_one)
    narrow_near, narrow_kept = near_second(me, send, near, narrow, near2, local_sem.at[5])
    arrive(far_one)
    narrow_far, narrow_far_kept = far_second(me, send, far, narrow, far2, local_sem.at[pl.ds(6, 2)])
    count(1)

    for n in range(3):
        arrive([second[n, hop] for hop in (1, 2, 3)])
        at = me[ORDERS[n][1]] * 4

        def add(i, carry):
            u[n][i] = t[n][at + i] + (r2[n][0, i] + r2[n][1, i] + r2[n][2, i])
            return carry

        lax.fori_loop(0, 4, add, 0)
        for hop in (1, 3, 2):
            to = (me[ORDERS[n][2]] + hop) % 4
            third[n, hop] = send(
                u[n].at[to], r3[n].at[hop - 1], sem3, (n, hop - 1), neighbour(me, **{ORDERS[n][2]: hop})
            )

    count(2)
    arrive([], wide_kept)
    near_turns(True, wide_near, NEAR_TURNS[7:])
    near_turns(True, wide_near, NEAR_TURNS[:4])
    far_turns(True, wide_far, wide_far_kept, 0)
    near_turns(True, wide_near, NEAR_TURNS[4:7])
    far_turns(True, wide_far, wide_far_kept, 1)
    arrive([], narrow_kept)
    near_turns(False, narrow_near, NEAR_TURNS[7:])
    near_turns(False, narrow_near, NEAR_TURNS[:4])
    far_turns(False, narrow_far, narrow_far_kept, 0)
    for n, (start, rows) in enumerate(BANDS):
        arrive([third[n, hop] for hop in (1, 2, 3)])
        total = u[n][me[ORDERS[n][2]]] + (r3[n][0] + r3[n][1] + r3[n][2])
        proj_ref[start : start + rows] = total * scale
    near_turns(False, narrow_near, NEAR_TURNS[4:7])
    far_turns(False, narrow_far, narrow_far_kept, 1)

    total = a3[...]
    high = total.astype(BF)
    rest = total - high.astype(F32)
    middle = rest.astype(BF)
    last = (rest - middle.astype(F32)).astype(BF)
    w = w_ref[W12:WSUM]
    widest = sum(lax.dot_general(part, w, MINOR, preferred_element_type=F32) for part in (last, middle, high))
    table_ref[...] = jnp.concatenate([a1[...], a2[...], widest], axis=1)
    for copy in remote:
        copy.wait_send()


def exchange(send, near_wide, far_wide, sums, lookups, lengths, weights, scale):
    total = lookups.shape[2]

    def each(*lead):
        return [pltpu.VMEM(lead + (rows, PD), F32) for _, rows in BANDS]

    count = send.shape[-1]
    return pl.pallas_call(
        functools.partial(exchange_kernel, scale),
        in_specs=[pl.BlockSpec(memory_space=pl.ANY)] * 3 + [pl.BlockSpec(memory_space=pltpu.VMEM)] * 6,
        out_specs=[pl.BlockSpec(memory_space=pltpu.VMEM)] * 2,
        out_shape=[
            jax.ShapeDtypeStruct((ROWS, WSUM), F32),
            jax.ShapeDtypeStruct((WSUM, PD), F32),
        ],
        scratch_shapes=[
            *each(3, 4),
            *each(4),
            *each(3),
            pltpu.VMEM((3, LOW, total), jnp.int32),
            pltpu.VMEM((2, 4, 8, W12, count), BF),
            pltpu.VMEM((2, 4, 2, 4, W12, count), BF),
            pltpu.VMEM((4, 4, 8, count, PD), BF),
            pltpu.VMEM((4, 4, 8, W12, count), BF),
            pltpu.VMEM((ROWS, W1), F32),
            pltpu.VMEM((ROWS, W2), F32),
            pltpu.VMEM((ROWS, PD), F32),
            pltpu.SemaphoreType.DMA((2, 3, 3)),
            pltpu.SemaphoreType.DMA((2, 3, 3)),
            pltpu.SemaphoreType.DMA((2, 2, 8)),
            pltpu.SemaphoreType.DMA((2, 2, 4)),
            pltpu.SemaphoreType.DMA((2, 2, 4)),
            pltpu.SemaphoreType.DMA((2, 2, 8)),
            pltpu.SemaphoreType.DMA((2, 2, 4)),
            pltpu.SemaphoreType.DMA((2, 2, 8)),
            pltpu.SemaphoreType.DMA((8,)),
        ],
        compiler_params=pltpu.CompilerParams(
            collective_id=0, has_side_effects=True, vmem_limit_bytes=62 * 2**20
        ),
        cost_estimate=pl.CostEstimate(flops=10**10, bytes_accessed=60 * 10**6, transcendentals=0),
    )(send, near_wide, far_wide, *sums, lookups, lengths, weights)


def local(grad_out, pooled, proj, assign, indices, lengths):
    scale = 1.0 / math.sqrt(grad_out.shape[0] * SLOTS)
    send, near, far, *sums = prepare(assign, proj[0], grad_out, pooled)
    lookups = jnp.transpose(indices[0], (1, 2, 0))
    table_grad, proj_grad = exchange(
        send, near, far, sums, lookups, jnp.transpose(lengths, (2, 0, 1)), proj[0], scale
    )
    return (table_grad[None], proj_grad[None])


def solution(mesh):
    placed = (
        P(("node", "local"), None, None),
        P(("node", "local"), None, None),
        P(("node", "local"), None, None),
        P(),
        P(("node", "local"), None, None, None),
        P(("node", "local"), None, None),
    )
    return jax.shard_map(
        local,
        mesh=mesh,
        in_specs=placed,
        out_specs=(P(("node", "local"), None, None), P(("node", "local"), None, None)),
        check_vma=False,
    )
```
